32 devices in a mesh: pipe: 4 (over z), ctx: 4 (over y, core), tp: 2 (over x).
Axes of the slice: x: 2, y: 2, z: 4, core: 2. Of those that a mesh axis runs over, the one named last changes fastest.
Arguments:
- queries: bfloat16 [4, 1024, 8192], P('pipe', 'ctx', 'tp'), may hold values from -16 to 16
- key_codes: bfloat16 [4, 1024, 512], P('pipe', 'ctx', 'tp'), may hold values from -127 to 127
- value_codes: bfloat16 [4, 1024, 512], P('pipe', 'ctx', 'tp'), may hold values from -127 to 127
- kv_scales: float32 [4, 8, 8], P('pipe', 'ctx'), may hold values from 0.004 to 0.032
- saved_out: bfloat16 [4, 1024, 8192], P('pipe', 'ctx', 'tp'), may hold values from -6 to 6
- section_grads: bfloat16 [4, 1024, 8192], P('pipe', 'ctx', 'tp'), may hold values from -6 to 6
- block_order: int32 [8], replicated, may hold values from 0 to 7, as said below
- block_docs: int32 [8], replicated, may hold values from 0 to 2, never falling along the last dimension, each value on 1 to 5 neighbouring positions
Outputs:
- grad_queries: bfloat16 [4, 1024, 8192], P('pipe', 'ctx', 'tp')
- grad_keys: bfloat16 [4, 1024, 512], P('pipe', ('ctx', 'tp'))
- grad_values: bfloat16 [4, 1024, 512], P('pipe', ('ctx', 'tp'))
The draws below stay inside these ranges and needn't reach their ends.
Inputs may be any that keep to these rules, and one draw needn't show every extreme that they name: `block_order`: a permutation of the 8 sequence blocks; stored blocks 2 d and 2 d + 1 are sequence blocks p and 7 - p for some p.
All inputs are finite; a program needn't handle non-finite values.
Results may differ from the reference program's by a relative error of at most 0.0072.
Values may be sent and summed in bfloat16 or wider, within the bound.
A program may use at most 192 MiB of HBM per device.

```python
import math
import jax
import jax.numpy as jnp
import numpy as np
from jax import lax

HQ = 64
KVH = 4
HD = 128
SECTIONS = 4
TOKENS = 1024
NB = 8
BLK = 128


def code_table(key, tie):
    shape = (SECTIONS, TOKENS, KVH * HD)
    codes = jax.random.randint(key, shape, -127, 128).astype(jnp.float32)
    rows = jnp.arange(TOKENS)
    target_rows = rows % BLK == BLK // 2 - 1
    columns = jnp.arange(KVH * HD)
    kept_column = columns % HD != HD - 1
    following = jnp.roll(codes, -1, axis=1)
    copy_here = target_rows[None, :, None] & kept_column[None, None, :] & (tie > 0.5)
    return jnp.where(copy_here, following, codes)


def draw_key_codes(key, part):
    codes = code_table(key, 0.0)
    return codes.astype(jnp.bfloat16)


def draw_queries(key, part):
    shape = (SECTIONS, TOKENS, HQ * HD)
    key = jax.random.fold_in(key, 3)
    values = jnp.clip(jax.random.normal(key, shape, jnp.float32), -6.0, 6.0)
    return values.astype(jnp.bfloat16)


def draw_value_codes(key, part):
    key = jax.random.fold_in(key, 7)
    codes = jax.random.randint(key, (SECTIONS, TOKENS, KVH * HD), -127, 128)
    return codes.astype(jnp.float32).astype(jnp.bfloat16)


def draw_kv_scales(key, part):
    key = jax.random.fold_in(key, 5)
    shape = (SECTIONS, NB, 2 * KVH)
    spread = jax.random.uniform(key, shape, jnp.float32, jnp.log(0.004), jnp.log(0.032))
    scales = jnp.exp(spread)
    return scales


def draw_block_order(key, part):
    key = jax.random.fold_in(key, 11)
    pairs = NB // 2
    chosen = jax.random.permutation(key, pairs).astype(jnp.int32)
    partner = (NB - 1 - chosen).astype(jnp.int32)
    return jnp.stack([chosen, partner], axis=1).reshape(NB)


def steps_of(rng, shape, shards, least, largest):
    factor_of = 1.0
    for axis_at, blocks in shards:
        draws = jax.random.uniform(jax.random.fold_in(jax.random.fold_in(rng, 6), axis_at), (blocks,), jnp.float32, least / len(shards), largest / len(shards))
        factor_of = factor_of * jnp.repeat(jnp.exp(draws), shape[axis_at] // blocks).reshape((-1,) + (1,) * (len(shape) - 1 - axis_at))
    return factor_of


def profile(count, total, bound, lean):
    weights = [(1 << 20) // math.isqrt(standing ** lean) + 1 for standing in range(2, count + 1)]
    surplus, given = total - bound - (count - 1), [1] * (count - 1)
    while surplus > 0:
        free = [i for i in range(count - 1) if given[i] < bound]
        mass, budget = sum([weights[i] for i in free]), surplus
        for i in free:
            addition = min(bound - given[i], max(1, budget * weights[i] // mass), surplus)
            given[i] = given[i] + addition
            surplus = surplus - addition
    return np.array([bound] + given)


def uneven(key, amount, total, reach, lean):
    if amount == 2:
        one = jax.random.randint(key, (), max(1, total - reach), min(reach, total - 1) + 1)
        return jnp.stack([one, total - one])
    lengths = jnp.asarray(profile(amount, total, reach, lean), jnp.int32)
    pairs = (amount - 1) // 2
    giver, taker = lengths[1:1 + 2 * pairs:2], lengths[2:2 + 2 * pairs:2]
    slack = jnp.minimum(giver - 1, reach - taker)
    shifted = jax.random.randint(jax.random.fold_in(key, 1), (pairs,), 0, 1 << 20) % (slack + 1)
    lengths = lengths.at[1:1 + 2 * pairs:2].set(giver - shifted).at[2:2 + 2 * pairs:2].set(taker + shifted)
    return lengths[jax.random.permutation(jax.random.fold_in(key, 2), amount)]


def noise(key, shape, scale, bound, shards=(), kind=jnp.bfloat16):
    values = scale * jax.random.normal(key, shape, jnp.float32)
    if shards:
        values = values * steps_of(key, shape, shards, -0.22, 0.18)
    return jnp.clip(values, -bound, bound).astype(kind)


def setup_inputs(seed: int = 0) -> dict:
    key_of = jax.random.split(jax.random.key(seed), 9)
    return {
        "queries": draw_queries(jax.random.fold_in(key_of[8], 71), 0),
        "key_codes": draw_key_codes(jax.random.fold_in(key_of[8], 71), 0),
        "value_codes": draw_value_codes(jax.random.fold_in(key_of[8], 71), 0),
        "kv_scales": draw_kv_scales(jax.random.fold_in(key_of[8], 71), 0),
        "saved_out": noise(key_of[4], (SECTIONS, TOKENS, HQ * HD), 1.0, 6.0, ((0, 4), (1, 4), (2, 2))),
        "section_grads": noise(key_of[5], (SECTIONS, TOKENS, HQ * HD), 1.0, 6.0, ((0, 4), (1, 4), (2, 2))),
        "block_order": draw_block_order(jax.random.fold_in(key_of[8], 71), 0),
        "block_docs": jnp.searchsorted(jnp.cumsum(uneven(key_of[7], 3, NB, NB // 2 + 1, 1)), jnp.arange(NB), side="right").astype(jnp.int32),
    }


masked_floor = -1.0e30


def section_backward(queries, key_codes, value_codes, scales, forward_out, grad_out, seq_blocks, positions, block_docs):
    inverse = HD ** -0.5
    repeats = HQ // KVH
    key_scale = jnp.repeat(scales[:, :KVH], BLK, axis=0)
    value_scale = jnp.repeat(scales[:, KVH:], BLK, axis=0)
    keys = (key_codes.astype(jnp.float32).reshape(TOKENS, KVH, HD) * key_scale[:, :, None]).astype(jnp.bfloat16)
    values = (value_codes.astype(jnp.float32).reshape(TOKENS, KVH, HD) * value_scale[:, :, None]).astype(jnp.bfloat16)
    documents = block_docs[seq_blocks]
    visible = (positions[None, :] <= positions[:, None]) & (documents[None, :] == documents[:, None])
    query_all = queries.reshape(TOKENS, KVH, repeats, HD)
    grad_all = grad_out.reshape(TOKENS, KVH, repeats, HD)
    out_all = forward_out.reshape(TOKENS, KVH, repeats, HD)
    highest = lax.Precision.HIGHEST

    def one_group(group):
        query = lax.dynamic_index_in_dim(query_all, group, 1, keepdims=False).astype(jnp.float32)
        grad_here = lax.dynamic_index_in_dim(grad_all, group, 1, keepdims=False).astype(jnp.float32)
        out_here = lax.dynamic_index_in_dim(out_all, group, 1, keepdims=False).astype(jnp.float32)
        key_here = lax.dynamic_index_in_dim(keys, group, 1, keepdims=False).astype(jnp.float32)
        value_here = lax.dynamic_index_in_dim(values, group, 1, keepdims=False).astype(jnp.float32)
        scores = jnp.einsum('ird,jd->rij', query, key_here, precision=highest) * inverse
        running_max = jnp.max(jnp.where(visible[None], scores, masked_floor), axis=-1)
        running_sum = jnp.sum(jnp.where(visible[None], jnp.exp(scores - running_max[..., None]), 0.0), axis=-1)
        log_norm = running_max + jnp.log(running_sum)
        probs = jnp.where(visible[None], jnp.exp(scores - log_norm[..., None]), 0.0)
        row_dots = jnp.transpose(jnp.sum(grad_here * out_here, axis=-1))
        dprobs = jnp.einsum('ird,jd->rij', grad_here, value_here, precision=highest)
        dscores = (probs * (dprobs - row_dots[:, :, None]) * inverse).astype(jnp.bfloat16)
        dscores = lax.optimization_barrier(dscores).astype(jnp.float32)
        probs_low = lax.optimization_barrier(probs.astype(jnp.bfloat16)).astype(jnp.float32)
        grad_query = jnp.einsum('rij,jd->ird', dscores, key_here, precision=highest)
        grad_key = jnp.einsum('rij,ird->jd', dscores, query, precision=highest)
        grad_value = jnp.einsum('rij,ird->jd', probs_low, grad_here, precision=highest)
        return grad_query, grad_key, grad_value

    grad_query, grad_key, grad_value = lax.map(one_group, jnp.arange(KVH, dtype=jnp.int32))
    grad_query = jnp.transpose(grad_query, (1, 0, 2, 3)).reshape(TOKENS, HQ * HD).astype(jnp.bfloat16)
    grad_key = jnp.transpose(grad_key, (1, 0, 2)).reshape(TOKENS, KVH * HD).astype(jnp.bfloat16)
    grad_value = jnp.transpose(grad_value, (1, 0, 2)).reshape(TOKENS, KVH * HD).astype(jnp.bfloat16)
    return grad_query, grad_key, grad_value


def reference(queries, key_codes, value_codes, kv_scales, saved_out, section_grads, block_order, block_docs):
    rows = jnp.arange(TOKENS, dtype=jnp.int32)
    seq_blocks = block_order[rows // BLK].astype(jnp.int32)
    positions = seq_blocks * BLK + rows % BLK
    incoming = jnp.roll(section_grads, -1, axis=0)
    query_list = []
    key_list = []
    value_list = []
    for section in range(SECTIONS):
        grad_query, grad_key, grad_value = section_backward(queries[section], key_codes[section], value_codes[section], kv_scales[section], saved_out[section], incoming[section], seq_blocks, positions, block_docs)
        query_list.append(grad_query)
        key_list.append(grad_key)
        value_list.append(grad_value)
    return jnp.stack(query_list), jnp.stack(key_list), jnp.stack(value_list)
```

```python
import jax
import jax.numpy as jnp
from jax import lax
from jax.experimental import pallas as pl
from jax.experimental.pallas import tpu as pltpu
from jax.sharding import PartitionSpec as P

HQ = 64
KVH = 4
HD = 128
HEADS_AT_ONCE = 2

masked_floor = -1e30
MESH = pl.DeviceIdType.MESH
NT = (((1,), (1,)), ((), ()))
NN = (((1,), (0,)), ((), ()))


def dot(a, b, dims=NN):
    return lax.dot_general(a, b, dims, preferred_element_type=jnp.float32)


def make_kernel(sizes, rows, heads, kv_here, blocks):
    pipes, cycle, tps = sizes
    blk = rows // 2
    width = HEADS_AT_ONCE * HD
    chunks = heads // HEADS_AT_ONCE
    per_kv = chunks // kv_here
    supers = blocks // 2
    sure = blocks // 4 + 1
    floats = supers - sure
    tasks = sure + 1 + floats
    peers = cycle * tps
    inverse = HD ** (-0.5)

    def kernel(
        order_ref, docs_ref, scales_ref, key_codes, value_codes, queries, saved, grads,
        dq_out, dk_out, dv_out,
        q_buf, o_buf, do_buf, dq_buf, k_all, v_all, k_seq, v_seq, kt_seq, bias, probs,
        dk_acc, dv_acc, send_buf, recv_buf,
        q_sem, o_sem, dq_sem, z_send, z_recv, kv_send, kv_recv, g_send, g_recv,
    ):
        pipe = lax.axis_index("pipe")
        ctx = lax.axis_index("ctx")
        tp = lax.axis_index("tp")
        me = ctx * tps + tp
        ahead = lax.rem(pipe + 1, pipes)
        behind = lax.rem(pipe + pipes - 1, pipes)

        def peer(k):
            flat = lax.rem(me + k, peers)
            return flat, (pipe, flat // tps, lax.rem(flat, tps))

        barrier = pltpu.get_barrier_semaphore()
        for where in (ahead, behind):
            pl.semaphore_signal(barrier, inc=1, device_id=(where, ctx, tp), device_id_type=MESH)
        for k in range(1, peers):
            pl.semaphore_signal(barrier, inc=1, device_id=peer(k)[1], device_id_type=MESH)
        pl.semaphore_wait(barrier, peers + 1)

        def columns(ref, c):
            return ref.at[0, :, pl.ds(pl.multiple_of(c * width, width), width)]

        def z_copy(c):
            return pltpu.make_async_remote_copy(
                src_ref=columns(grads, c), dst_ref=do_buf.at[c],
                send_sem=z_send.at[c], recv_sem=z_recv.at[c],
                device_id=(behind, ctx, tp), device_id_type=MESH,
            )

        def q_copy(c):
            return pltpu.make_async_copy(columns(queries, c), q_buf.at[c], q_sem.at[c])

        def o_copy(c):
            return pltpu.make_async_copy(columns(saved, c), o_buf.at[c], o_sem.at[c])

        def dq_copy(c):
            return pltpu.make_async_copy(dq_buf.at[c], columns(dq_out, c), dq_sem.at[c])

        @pl.loop(0, chunks)
        def _(c):
            z_copy(c).start()

        @pl.loop(0, chunks)
        def _(c):
            q_copy(c).start()

        here = pl.ds(2 * ctx, 2)
        gathered = (k_all, v_all)
        for kind, codes in ((0, key_codes), (1, value_codes)):
            for half in range(2):
                for g in range(kv_here):
                    scale = scales_ref[0, half, kind * KVH + tp * kv_here + g]
                    piece = codes[0, half * blk:(half + 1) * blk, g * HD:(g + 1) * HD]
                    gathered[kind][2 * ctx + half, :, g * HD:(g + 1) * HD] = (
                        piece.astype(jnp.float32) * scale
                    ).astype(jnp.bfloat16)

        def kv_copy(kind, k):
            return pltpu.make_async_remote_copy(
                src_ref=gathered[kind].at[here], dst_ref=gathered[kind].at[here],
                send_sem=kv_send.at[kind, k], recv_sem=kv_recv.at[kind, k],
                device_id=(pipe, lax.rem(ctx + k, cycle), tp), device_id_type=MESH,
            )

        for kind in range(2):
            for k in range(1, cycle):
                kv_copy(kind, k).start()

        @pl.loop(0, chunks)
        def _(c):
            o_copy(c).start()

        first = order_ref[2 * ctx]
        second = order_ref[2 * ctx + 1]
        first_hi = jnp.minimum(jnp.maximum(first - second, 0), 1)
        hi_block = jnp.maximum(first, second)
        lo_block = jnp.minimum(first, second)
        lo_count = lax.div(lo_block + 2, 2)

        float_hi, float_super = [], []
        for f in range(floats):
            is_hi = jnp.minimum(jnp.maximum(f + 2 - lo_count, 0), 1)
            float_hi.append(is_hi)
            float_super.append(jnp.clip(1 + f + is_hi * (sure - lo_count), 0, supers - 1))

        def choose(flag, one, other):
            return jnp.where(jnp.full(one.shape, flag, jnp.int32) > 0, one, other)

        def super_of(t):
            if t < sure:
                return t
            return 0 if t == sure else float_super[t - sure - 1]

        def pick(t, hi, lo):
            if t < sure:
                return hi
            if t == sure:
                return lo
            flag = float_hi[t - sure - 1]
            if hi.shape == ():
                return flag * hi + (1 - flag) * lo
            return choose(flag, hi, lo)

        for t in range(tasks):
            m = super_of(t)
            block = pick(t, hi_block, lo_block)
            key = lax.broadcasted_iota(jnp.int32, (2 * blk, width), 0)
            row = lax.broadcasted_iota(jnp.int32, (2 * blk, width), 1) % HD
            key_doc = jnp.where(key < blk, docs_ref[2 * m], docs_ref[2 * m + 1])
            seen = (key - row <= block * blk - m * (2 * blk)) & (key_doc == docs_ref[block])
            bias[t] = jnp.where(seen, 0.0, masked_floor)

        def stored_at(b):
            place = jnp.int32(0)
            for r in range(blocks):
                place = place + r * (1 - jnp.minimum(jnp.abs(order_ref[r] - b), 1))
            return jnp.minimum(place, blocks - 1)

        def sort_blocks(kind, seq):
            for k in range(1, cycle):
                kv_copy(kind, k).wait_recv()
            for b in range(blocks):
                piece = gathered[kind][stored_at(b)]
                for g in range(kv_here):
                    part = piece[:, g * HD:(g + 1) * HD]
                    lanes = pl.ds((b % 2) * blk, blk)
                    seq[g, b // 2, lanes, :] = part
                    if kind == 0:
                        turned = part.astype(jnp.float32).T.astype(jnp.bfloat16)
                        kt_seq[g, b // 2, :, lanes] = turned

        def stacked(buf, c):
            halves = []
            for half in range(2):
                piece = buf[c, half * blk:(half + 1) * blk, :]
                halves.append(jnp.concatenate(
                    [piece[:, h * HD:(h + 1) * HD] for h in range(HEADS_AT_ONCE)], axis=0
                ))
            return choose(first_hi, *halves), choose(first_hi, *halves[::-1])

        def combine(values, op, empty):
            hi, lo = None, values[sure]
            for t in range(sure):
                hi = values[t] if hi is None else op(hi, values[t])
            for f in range(floats):
                value = values[sure + 1 + f]
                hi = op(hi, choose(float_hi[f], value, empty))
                lo = op(lo, choose(1 - float_hi[f], value, empty))
            return hi, lo

        sort_blocks(0, k_seq)

        @pl.loop(0, chunks)
        def _(c):
            q_copy(c).wait()
            g = c // per_kv
            hi_query, lo_query = stacked(q_buf, c)
            scores, tops = [], []
            for t in range(tasks):
                query = pick(t, hi_query, lo_query)
                s = dot(k_seq[g, super_of(t)], query, NT) * inverse + bias[t]
                scores.append(s)
                tops.append(jnp.max(s, axis=0, keepdims=True))
            hi_top, lo_top = combine(tops, jnp.maximum, masked_floor)
            weights = [jnp.exp(scores[t] - pick(t, hi_top, lo_top)) for t in range(tasks)]
            sums = [jnp.sum(w, axis=0, keepdims=True) for w in weights]
            hi_sum, lo_sum = combine(sums, jnp.add, 0.0)
            hi_over, lo_over = 1.0 / hi_sum, 1.0 / lo_sum
            for t in range(tasks):
                probs[c, t] = (weights[t] * pick(t, hi_over, lo_over)).astype(jnp.bfloat16)

        sort_blocks(1, v_seq)

        @pl.loop(0, chunks)
        def _(c):
            o_copy(c).wait()

        def block_copy(g, k):
            flat, device = peer(k)
            return pltpu.make_async_remote_copy(
                src_ref=send_buf.at[g, flat], dst_ref=recv_buf.at[g, me],
                send_sem=g_send.at[g, k], recv_sem=g_recv.at[g, k],
                device_id=device, device_id_type=MESH,
            )

        for g in range(kv_here):
            dk_acc[...] = jnp.zeros_like(dk_acc)
            dv_acc[...] = jnp.zeros_like(dv_acc)

            @pl.loop(g * per_kv, (g + 1) * per_kv)
            def _(c):
                z_copy(c).wait_recv()

                dots = []
                for half in range(2):
                    here_rows = slice(half * blk, (half + 1) * blk)
                    both = do_buf[c, here_rows, :].astype(jnp.float32) * o_buf[
                        c, here_rows, :
                    ].astype(jnp.float32)
                    dots.append(jnp.concatenate([
                        jnp.sum(both[:, h * HD:(h + 1) * HD].T, axis=0, keepdims=True)
                        for h in range(HEADS_AT_ONCE)
                    ], axis=1))
                hi_dots, lo_dots = choose(first_hi, *dots), choose(first_hi, *dots[::-1])
                hi_query, lo_query = stacked(q_buf, c)
                hi_grad, lo_grad = stacked(do_buf, c)
                turned = []
                for t in range(tasks):
                    m = super_of(t)
                    query = pick(t, hi_query, lo_query)
                    grad = pick(t, hi_grad, lo_grad)
                    low = probs[c, t]
                    dp = dot(v_seq[g, m], grad, NT) - pick(t, hi_dots, lo_dots)
                    ds = (low.astype(jnp.float32) * dp).astype(jnp.bfloat16)
                    slot = t if t < sure else (0 if t == sure else supers + t - sure - 1)
                    dv_acc[2 * slot:2 * slot + 2] += dot(low, grad).reshape(2, blk, HD)
                    dk_acc[2 * slot:2 * slot + 2] += dot(ds, query).reshape(2, blk, HD)
                    turned.append(dot(kt_seq[g, m], ds))
                hi_turned, lo_turned = combine(turned, jnp.add, 0.0)
                top = choose(first_hi, hi_turned, lo_turned) * inverse
                low_half = choose(first_hi, lo_turned, hi_turned) * inverse
                for h in range(HEADS_AT_ONCE):
                    cols = slice(h * HD, (h + 1) * HD)
                    dq_buf[c, 0:blk, cols] = top[:, cols].T.astype(jnp.bfloat16)
                    dq_buf[c, blk:2 * blk, cols] = low_half[:, cols].T.astype(jnp.bfloat16)
                dq_copy(c).start()

            for kind, acc in ((0, dk_acc), (1, dv_acc)):
                for f in range(floats):
                    extra = acc[2 * (supers + f):2 * (supers + f) + 2]
                    for m in range(supers):
                        hit = 1 - jnp.minimum(jnp.abs(float_super[f] - m), 1)
                        acc[2 * m:2 * m + 2] += choose(hit, extra, 0.0)
                for r in range(blocks):
                    piece = acc[order_ref[r]]
                    send_buf[g, r, kind * blk:(kind + 1) * blk, :] = piece.astype(jnp.bfloat16)
            recv_buf[g, me] = send_buf[g, me]
            for k in range(1, peers):
                block_copy(g, k).start()

        for g in range(kv_here):
            for k in range(1, peers):
                block_copy(g, k).wait_recv()
            for t in range(tps):
                total = recv_buf[g, t].astype(jnp.float32)
                for d in range(1, cycle):
                    total = total + recv_buf[g, d * tps + t].astype(jnp.float32)
                cols = slice((t * kv_here + g) * HD, (t * kv_here + g + 1) * HD)
                dk_out[0, :, cols] = (total[:blk] * inverse).astype(jnp.bfloat16)
                dv_out[0, :, cols] = total[blk:].astype(jnp.bfloat16)

        @pl.loop(0, chunks)
        def _(c):
            z_copy(c).wait_send()
            dq_copy(c).wait()

        for kind in range(2):
            for k in range(1, cycle):
                kv_copy(kind, k).wait_send()
        for g in range(kv_here):
            for k in range(1, peers):
                block_copy(g, k).wait_send()

    bf16, f32 = jnp.bfloat16, jnp.float32
    scratch = [
        pltpu.VMEM((chunks, rows, width), bf16),
        pltpu.VMEM((chunks, rows, width), bf16),
        pltpu.VMEM((chunks, rows, width), bf16),
        pltpu.VMEM((chunks, rows, width), bf16),
        pltpu.VMEM((blocks, blk, kv_here * HD), bf16),
        pltpu.VMEM((blocks, blk, kv_here * HD), bf16),
        pltpu.VMEM((kv_here, supers, 2 * blk, HD), bf16),
        pltpu.VMEM((kv_here, supers, 2 * blk, HD), bf16),
        pltpu.VMEM((kv_here, supers, HD, 2 * blk), bf16),
        pltpu.VMEM((tasks, 2 * blk, width), f32),
        pltpu.VMEM((chunks, tasks, 2 * blk, width), bf16),
        pltpu.VMEM((2 * (supers + floats), blk, HD), f32),
        pltpu.VMEM((2 * (supers + floats), blk, HD), f32),
        pltpu.VMEM((kv_here, peers, 2 * blk, HD), bf16),
        pltpu.VMEM((kv_here, peers, 2 * blk, HD), bf16),
        pltpu.SemaphoreType.DMA((chunks,)),
        pltpu.SemaphoreType.DMA((chunks,)),
        pltpu.SemaphoreType.DMA((chunks,)),
        pltpu.SemaphoreType.DMA((chunks,)),
        pltpu.SemaphoreType.DMA((chunks,)),
        pltpu.SemaphoreType.DMA((2, cycle)),
        pltpu.SemaphoreType.DMA((2, cycle)),
        pltpu.SemaphoreType.DMA((kv_here, peers)),
        pltpu.SemaphoreType.DMA((kv_here, peers)),
    ]
    pairs = heads * tasks * 2 * blk * blk
    smem = pl.BlockSpec(memory_space=pltpu.SMEM)
    vmem = pl.BlockSpec(memory_space=pltpu.VMEM)
    hbm = pl.BlockSpec(memory_space=pl.ANY)
    return pl.pallas_call(
        kernel,
        out_shape=(
            jax.ShapeDtypeStruct((1, rows, heads * HD), bf16),
            jax.ShapeDtypeStruct((1, rows // tps, KVH * HD), bf16),
            jax.ShapeDtypeStruct((1, rows // tps, KVH * HD), bf16),
        ),
        in_specs=[smem, smem, smem, vmem, vmem, hbm, hbm, hbm],
        out_specs=(hbm, vmem, vmem),
        scratch_shapes=scratch,
        compiler_params=pltpu.CompilerParams(
            collective_id=0, has_side_effects=True, vmem_limit_bytes=56 << 20
        ),
        cost_estimate=pl.CostEstimate(
            flops=5 * 2 * HD * pairs, bytes_accessed=5 * rows * heads * HD * 2,
            transcendentals=pairs,
        ),
    )


def solution(mesh):
    sizes = (mesh.shape["pipe"], mesh.shape["ctx"], mesh.shape["tp"])

    def on_device(
        queries, key_codes, value_codes, kv_scales, saved_out, section_grads, block_order, block_docs
    ):
        call = make_kernel(
            sizes, queries.shape[1], queries.shape[2] // HD, key_codes.shape[2] // HD,
            block_order.shape[0],
        )
        return call(
            block_order, block_docs, kv_scales, key_codes, value_codes, queries, saved_out,
            section_grads,
        )

    in_specs = (
        P("pipe", "ctx", "tp"),
        P("pipe", "ctx", "tp"),
        P("pipe", "ctx", "tp"),
        P("pipe", "ctx", None),
        P("pipe", "ctx", "tp"),
        P("pipe", "ctx", "tp"),
        P(),
        P(),
    )
    out_specs = (
        P("pipe", "ctx", "tp"),
        P("pipe", ("ctx", "tp"), None),
        P("pipe", ("ctx", "tp"), None),
    )
    return jax.shard_map(
        on_device, mesh=mesh, in_specs=in_specs, out_specs=out_specs, check_vma=False
    )
```

```python
import jax
import jax.numpy as jnp
from jax import lax
from jax.experimental import pallas as pl
from jax.experimental.pallas import tpu as pltpu
from jax.sharding import PartitionSpec as P

HQ = 64
KVH = 4
HD = 128
HEADS_AT_ONCE = 2
IN_FLIGHT = 4

masked_floor = -1e30
MESH = pl.DeviceIdType.MESH
NT = (((1,), (1,)), ((), ()))
NN = (((1,), (0,)), ((), ()))


def dot(a, b, dims=NN):
    return lax.dot_general(a, b, dims, preferred_element_type=jnp.float32)


def make_kernel(sizes, rows, heads, kv_here, blocks):
    pipes, cycle, tps = sizes
    blk = rows // 2
    width = HEADS_AT_ONCE * HD
    chunks = heads // HEADS_AT_ONCE
    per_kv = chunks // kv_here
    in_flight = min(chunks, IN_FLIGHT)
    supers = blocks // 2
    sure = blocks // 4 + 1
    floats = supers - sure
    tasks = sure + 1 + floats
    peers = cycle * tps
    inverse = HD ** (-0.5)

    def kernel(
        order_ref, docs_ref, scales_ref, key_codes, value_codes, queries, saved, grads,
        dq_out, dk_out, dv_out,
        q_buf, o_buf, do_buf, dq_buf, k_all, v_all, k_seq, v_seq, kt_seq, bias, probs,
        dk_acc, dv_acc, send_buf, recv_buf,
        q_sem, o_sem, dq_sem, z_send, z_recv, kv_send, kv_recv, g_send, g_recv,
    ):
        pipe = lax.axis_index("pipe")
        ctx = lax.axis_index("ctx")
        tp = lax.axis_index("tp")
        me = ctx * tps + tp
        ahead = lax.rem(pipe + 1, pipes)
        behind = lax.rem(pipe + pipes - 1, pipes)

        def peer(k):
            flat = lax.rem(me + k, peers)
            return flat, (pipe, flat // tps, lax.rem(flat, tps))

        barrier = pltpu.get_barrier_semaphore()
        for where in (ahead, behind):
            pl.semaphore_signal(barrier, inc=1, device_id=(where, ctx, tp), device_id_type=MESH)
        for k in range(1, peers):
            pl.semaphore_signal(barrier, inc=1, device_id=peer(k)[1], device_id_type=MESH)
        pl.semaphore_wait(barrier, peers + 1)

        def columns(ref, c):
            return ref.at[0, :, pl.ds(pl.multiple_of(c * width, width), width)]

        def z_copy(c):
            return pltpu.make_async_remote_copy(
                src_ref=columns(grads, c), dst_ref=do_buf.at[c],
                send_sem=z_send.at[c], recv_sem=z_recv.at[c],
                device_id=(behind, ctx, tp), device_id_type=MESH,
            )

        def q_copy(c):
            return pltpu.make_async_copy(columns(queries, c), q_buf.at[c], q_sem.at[c])

        def o_copy(c):
            return pltpu.make_async_copy(columns(saved, c), o_buf.at[c], o_sem.at[c])

        def dq_copy(c):
            return pltpu.make_async_copy(dq_buf.at[c], columns(dq_out, c), dq_sem.at[c])

        @pl.loop(0, in_flight)
        def _(c):
            z_copy(c).start()

        @pl.loop(0, chunks)
        def _(c):
            q_copy(c).start()

        here = pl.ds(2 * ctx, 2)
        gathered = (k_all, v_all)
        for kind, codes in ((0, key_codes), (1, value_codes)):
            for half in range(2):
                for g in range(kv_here):
                    scale = scales_ref[0, half, kind * KVH + tp * kv_here + g]
                    piece = codes[0, half * blk:(half + 1) * blk, g * HD:(g + 1) * HD]
                    gathered[kind][2 * ctx + half, :, g * HD:(g + 1) * HD] = (
                        piece.astype(jnp.float32) * scale
                    ).astype(jnp.bfloat16)

        def kv_copy(kind, k):
            return pltpu.make_async_remote_copy(
                src_ref=gathered[kind].at[here], dst_ref=gathered[kind].at[here],
                send_sem=kv_send.at[kind, k], recv_sem=kv_recv.at[kind, k],
                device_id=(pipe, lax.rem(ctx + k, cycle), tp), device_id_type=MESH,
            )

        for kind in range(2):
            for k in range(1, cycle):
                kv_copy(kind, k).start()

        @pl.loop(0, chunks)
        def _(c):
            o_copy(c).start()

        first = order_ref[2 * ctx]
        second = order_ref[2 * ctx + 1]
        first_hi = jnp.minimum(jnp.maximum(first - second, 0), 1)
        hi_block = jnp.maximum(first, second)
        lo_block = jnp.minimum(first, second)
        lo_count = lax.div(lo_block + 2, 2)

        float_hi, float_super = [], []
        for f in range(floats):
            is_hi = jnp.minimum(jnp.maximum(f + 2 - lo_count, 0), 1)
            float_hi.append(is_hi)
            float_super.append(jnp.clip(1 + f + is_hi * (sure - lo_count), 0, supers - 1))

        def choose(flag, one, other):
            return jnp.where(jnp.full(one.shape, flag, jnp.int32) > 0, one, other)

        def super_of(t):
            if t < sure:
                return t
            return 0 if t == sure else float_super[t - sure - 1]

        def pick(t, hi, lo):
            if t < sure:
                return hi
            if t == sure:
                return lo
            flag = float_hi[t - sure - 1]
            if hi.shape == ():
                return flag * hi + (1 - flag) * lo
            return choose(flag, hi, lo)

        for t in range(tasks):
            m = super_of(t)
            block = pick(t, hi_block, lo_block)
            key = lax.broadcasted_iota(jnp.int32, (2 * blk, width), 0)
            row = lax.broadcasted_iota(jnp.int32, (2 * blk, width), 1) % HD
            key_doc = jnp.where(key < blk, docs_ref[2 * m], docs_ref[2 * m + 1])
            seen = (key - row <= block * blk - m * (2 * blk)) & (key_doc == docs_ref[block])
            bias[t] = jnp.where(seen, 0.0, masked_floor)

        def stored_at(b):
            place = jnp.int32(0)
            for r in range(blocks):
                place = place + r * (1 - jnp.minimum(jnp.abs(order_ref[r] - b), 1))
            return jnp.minimum(place, blocks - 1)

        def sort_blocks(kind, seq):
            for k in range(1, cycle):
                kv_copy(kind, k).wait_recv()
            for b in range(blocks):
                piece = gathered[kind][stored_at(b)]
                for g in range(kv_here):
                    part = piece[:, g * HD:(g + 1) * HD]
                    lanes = pl.ds((b % 2) * blk, blk)
                    seq[g, b // 2, lanes, :] = part
                    if kind == 0:
                        turned = part.astype(jnp.float32).T.astype(jnp.bfloat16)
                        kt_seq[g, b // 2, :, lanes] = turned

        def stacked(buf, c):
            halves = []
            for half in range(2):
                piece = buf[c, half * blk:(half + 1) * blk, :]
                halves.append(jnp.concatenate(
                    [piece[:, h * HD:(h + 1) * HD] for h in range(HEADS_AT_ONCE)], axis=0
                ))
            return choose(first_hi, *halves), choose(first_hi, *halves[::-1])

        def combine(values, op, empty):
            hi, lo = None, values[sure]
            for t in range(sure):
                hi = values[t] if hi is None else op(hi, values[t])
            for f in range(floats):
                value = values[sure + 1 + f]
                hi = op(hi, choose(float_hi[f], value, empty))
                lo = op(lo, choose(1 - float_hi[f], value, empty))
            return hi, lo

        sort_blocks(0, k_seq)

        @pl.loop(0, chunks)
        def _(c):
            q_copy(c).wait()
            g = c // per_kv
            hi_query, lo_query = stacked(q_buf, c)
            scores, tops = [], []
            for t in range(tasks):
                query = pick(t, hi_query, lo_query)
                s = dot(k_seq[g, super_of(t)], query, NT) * inverse + bias[t]
                scores.append(s)
                tops.append(jnp.max(s, axis=0, keepdims=True))
            hi_top, lo_top = combine(tops, jnp.maximum, masked_floor)
            weights = [jnp.exp(scores[t] - pick(t, hi_top, lo_top)) for t in range(tasks)]
            sums = [jnp.sum(w, axis=0, keepdims=True) for w in weights]
            hi_sum, lo_sum = combine(sums, jnp.add, 0.0)
            hi_over, lo_over = 1.0 / hi_sum, 1.0 / lo_sum
            for t in range(tasks):
                probs[c, t] = (weights[t] * pick(t, hi_over, lo_over)).astype(jnp.bfloat16)

        sort_blocks(1, v_seq)

        @pl.loop(0, chunks)
        def _(c):
            o_copy(c).wait()

        def block_copy(g, k):
            flat, device = peer(k)
            return pltpu.make_async_remote_copy(
                src_ref=send_buf.at[g, flat], dst_ref=recv_buf.at[g, me],
                send_sem=g_send.at[g, k], recv_sem=g_recv.at[g, k],
                device_id=device, device_id_type=MESH,
            )

        for g in range(kv_here):
            dk_acc[...] = jnp.zeros_like(dk_acc)
            dv_acc[...] = jnp.zeros_like(dv_acc)

            @pl.loop(g * per_kv, (g + 1) * per_kv)
            def _(c):
                z_copy(c).wait_recv()
                z_copy(c).wait_send()

                @pl.when(c + in_flight < chunks)
                def _():
                    z_copy(c + in_flight).start()

                dots = []
                for half in range(2):
                    here_rows = slice(half * blk, (half + 1) * blk)
                    both = do_buf[c, here_rows, :].astype(jnp.float32) * o_buf[
                        c, here_rows, :
                    ].astype(jnp.float32)
                    dots.append(jnp.concatenate([
                        jnp.sum(both[:, h * HD:(h + 1) * HD].T, axis=0, keepdims=True)
                        for h in range(HEADS_AT_ONCE)
                    ], axis=1))
                hi_dots, lo_dots = choose(first_hi, *dots), choose(first_hi, *dots[::-1])
                hi_query, lo_query = stacked(q_buf, c)
                hi_grad, lo_grad = stacked(do_buf, c)
                turned = []
                for t in range(tasks):
                    m = super_of(t)
                    query = pick(t, hi_query, lo_query)
                    grad = pick(t, hi_grad, lo_grad)
                    low = probs[c, t]
                    dp = dot(v_seq[g, m], grad, NT) - pick(t, hi_dots, lo_dots)
                    ds = (low.astype(jnp.float32) * dp).astype(jnp.bfloat16)
                    slot = t if t < sure else (0 if t == sure else supers + t - sure - 1)
                    dv_acc[2 * slot:2 * slot + 2] += dot(low, grad).reshape(2, blk, HD)
                    dk_acc[2 * slot:2 * slot + 2] += dot(ds, query).reshape(2, blk, HD)
                    turned.append(dot(kt_seq[g, m], ds))
                hi_turned, lo_turned = combine(turned, jnp.add, 0.0)
                top = choose(first_hi, hi_turned, lo_turned) * inverse
                low_half = choose(first_hi, lo_turned, hi_turned) * inverse
                for h in range(HEADS_AT_ONCE):
                    cols = slice(h * HD, (h + 1) * HD)
                    dq_buf[c, 0:blk, cols] = top[:, cols].T.astype(jnp.bfloat16)
                    dq_buf[c, blk:2 * blk, cols] = low_half[:, cols].T.astype(jnp.bfloat16)
                dq_copy(c).start()

            for kind, acc in ((0, dk_acc), (1, dv_acc)):
                for f in range(floats):
                    extra = acc[2 * (supers + f):2 * (supers + f) + 2]
                    for m in range(supers):
                        hit = 1 - jnp.minimum(jnp.abs(float_super[f] - m), 1)
                        acc[2 * m:2 * m + 2] += choose(hit, extra, 0.0)
                for r in range(blocks):
                    piece = acc[order_ref[r]]
                    send_buf[g, r, kind * blk:(kind + 1) * blk, :] = piece.astype(jnp.bfloat16)
            recv_buf[g, me] = send_buf[g, me]
            for k in range(1, peers):
                block_copy(g, k).start()

        for g in range(kv_here):
            for k in range(1, peers):
                block_copy(g, k).wait_recv()
            for t in range(tps):
                total = recv_buf[g, t].astype(jnp.float32)
                for d in range(1, cycle):
                    total = total + recv_buf[g, d * tps + t].astype(jnp.float32)
                cols = slice((t * kv_here + g) * HD, (t * kv_here + g + 1) * HD)
                dk_out[0, :, cols] = (total[:blk] * inverse).astype(jnp.bfloat16)
                dv_out[0, :, cols] = total[blk:].astype(jnp.bfloat16)

        @pl.loop(0, chunks)
        def _(c):
            dq_copy(c).wait()

        for kind in range(2):
            for k in range(1, cycle):
                kv_copy(kind, k).wait_send()
        for g in range(kv_here):
            for k in range(1, peers):
                block_copy(g, k).wait_send()

    bf16, f32 = jnp.bfloat16, jnp.float32
    scratch = [
        pltpu.VMEM((chunks, rows, width), bf16),
        pltpu.VMEM((chunks, rows, width), bf16),
        pltpu.VMEM((chunks, rows, width), bf16),
        pltpu.VMEM((chunks, rows, width), bf16),
        pltpu.VMEM((blocks, blk, kv_here * HD), bf16),
        pltpu.VMEM((blocks, blk, kv_here * HD), bf16),
        pltpu.VMEM((kv_here, supers, 2 * blk, HD), bf16),
        pltpu.VMEM((kv_here, supers, 2 * blk, HD), bf16),
        pltpu.VMEM((kv_here, supers, HD, 2 * blk), bf16),
        pltpu.VMEM((tasks, 2 * blk, width), f32),
        pltpu.VMEM((chunks, tasks, 2 * blk, width), bf16),
        pltpu.VMEM((2 * (supers + floats), blk, HD), f32),
        pltpu.VMEM((2 * (supers + floats), blk, HD), f32),
        pltpu.VMEM((kv_here, peers, 2 * blk, HD), bf16),
        pltpu.VMEM((kv_here, peers, 2 * blk, HD), bf16),
        pltpu.SemaphoreType.DMA((chunks,)),
        pltpu.SemaphoreType.DMA((chunks,)),
        pltpu.SemaphoreType.DMA((chunks,)),
        pltpu.SemaphoreType.DMA((chunks,)),
        pltpu.SemaphoreType.DMA((chunks,)),
        pltpu.SemaphoreType.DMA((2, cycle)),
        pltpu.SemaphoreType.DMA((2, cycle)),
        pltpu.SemaphoreType.DMA((kv_here, peers)),
        pltpu.SemaphoreType.DMA((kv_here, peers)),
    ]
    pairs = heads * tasks * 2 * blk * blk
    smem = pl.BlockSpec(memory_space=pltpu.SMEM)
    vmem = pl.BlockSpec(memory_space=pltpu.VMEM)
    hbm = pl.BlockSpec(memory_space=pl.ANY)
    return pl.pallas_call(
        kernel,
        out_shape=(
            jax.ShapeDtypeStruct((1, rows, heads * HD), bf16),
            jax.ShapeDtypeStruct((1, rows // tps, KVH * HD), bf16),
            jax.ShapeDtypeStruct((1, rows // tps, KVH * HD), bf16),
        ),
        in_specs=[smem, smem, smem, vmem, vmem, hbm, hbm, hbm],
        out_specs=(hbm, vmem, vmem),
        scratch_shapes=scratch,
        compiler_params=pltpu.CompilerParams(
            collective_id=0, has_side_effects=True, vmem_limit_bytes=56 << 20
        ),
        cost_estimate=pl.CostEstimate(
            flops=5 * 2 * HD * pairs, bytes_accessed=5 * rows * heads * HD * 2,
            transcendentals=pairs,
        ),
    )


def solution(mesh):
    sizes = (mesh.shape["pipe"], mesh.shape["ctx"], mesh.shape["tp"])

    def on_device(
        queries, key_codes, value_codes, kv_scales, saved_out, section_grads, block_order, block_docs
    ):
        call = make_kernel(
            sizes, queries.shape[1], queries.shape[2] // HD, key_codes.shape[2] // HD,
            block_order.shape[0],
        )
        return call(
            block_order, block_docs, kv_scales, key_codes, value_codes, queries, saved_out,
            section_grads,
        )

    in_specs = (
        P("pipe", "ctx", "tp"),
        P("pipe", "ctx", "tp"),
        P("pipe", "ctx", "tp"),
        P("pipe", "ctx", None),
        P("pipe", "ctx", "tp"),
        P("pipe", "ctx", "tp"),
        P(),
        P(),
    )
    out_specs = (
        P("pipe", "ctx", "tp"),
        P("pipe", ("ctx", "tp"), None),
        P("pipe", ("ctx", "tp"), None),
    )
    return jax.shard_map(
        on_device, mesh=mesh, in_specs=in_specs, out_specs=out_specs, check_vma=False
    )
```

```python
import jax
import jax.numpy as jnp
from jax import lax
from jax.experimental import pallas as pl
from jax.experimental.pallas import tpu as pltpu
from jax.sharding import PartitionSpec as P

HQ = 64
KVH = 4
HD = 128
HEADS_AT_ONCE = 2
IN_FLIGHT = 6
LEAD = 2

masked_floor = -1e30
MESH = pl.DeviceIdType.MESH
NT = (((1,), (1,)), ((), ()))
NN = (((1,), (0,)), ((), ()))


def dot(a, b, dims=NN):
    return lax.dot_general(a, b, dims, preferred_element_type=jnp.float32)


def make_kernel(sizes, rows, heads, kv_here, blocks):
    pipes, cycle, tps = sizes
    blk = rows // 2
    width = HEADS_AT_ONCE * HD
    chunks = heads // HEADS_AT_ONCE
    per_kv = chunks // kv_here
    in_flight, lead = min(chunks, IN_FLIGHT), min(chunks, LEAD)
    supers = blocks // 2
    sure = blocks // 4 + 1
    floats = supers - sure
    tasks = sure + 1 + floats
    peers = cycle * tps
    inverse = HD ** (-0.5)

    def kernel(
        order_ref, docs_ref, scales_ref, key_codes, value_codes, queries, saved, grads,
        dq_out, dk_out, dv_out,
        q_buf, o_buf, do_buf, dq_buf, k_all, v_all, k_seq, v_seq, kt_seq, bias, probs,
        dk_acc, dv_acc, send_buf, recv_buf,
        q_sem, o_sem, dq_sem, z_send, z_recv, kv_send, kv_recv, g_send, g_recv,
    ):
        pipe = lax.axis_index("pipe")
        ctx = lax.axis_index("ctx")
        tp = lax.axis_index("tp")
        me = ctx * tps + tp
        ahead = lax.rem(pipe + 1, pipes)
        behind = lax.rem(pipe + pipes - 1, pipes)

        def peer(k):
            flat = lax.rem(me + k, peers)
            return flat, (pipe, flat // tps, lax.rem(flat, tps))

        barrier = pltpu.get_barrier_semaphore()
        for where in (ahead, behind):
            pl.semaphore_signal(barrier, inc=1, device_id=(where, ctx, tp), device_id_type=MESH)
        for k in range(1, peers):
            pl.semaphore_signal(barrier, inc=1, device_id=peer(k)[1], device_id_type=MESH)
        pl.semaphore_wait(barrier, peers + 1)

        def columns(ref, c):
            return ref.at[0, :, pl.ds(pl.multiple_of(c * width, width), width)]

        def z_copy(c):
            return pltpu.make_async_remote_copy(
                src_ref=columns(grads, c), dst_ref=do_buf.at[c],
                send_sem=z_send.at[c], recv_sem=z_recv.at[c],
                device_id=(behind, ctx, tp), device_id_type=MESH,
            )

        def q_copy(c):
            return pltpu.make_async_copy(columns(queries, c), q_buf.at[c], q_sem.at[c])

        def o_copy(c):
            return pltpu.make_async_copy(columns(saved, c), o_buf.at[c], o_sem.at[c])

        def dq_copy(c):
            return pltpu.make_async_copy(dq_buf.at[c], columns(dq_out, c), dq_sem.at[c])

        @pl.loop(0, in_flight)
        def _(c):
            z_copy(c).start()

        @pl.loop(0, chunks)
        def _(c):
            q_copy(c).start()

        here = pl.ds(2 * ctx, 2)
        gathered = (k_all, v_all)
        for kind, codes in ((0, key_codes), (1, value_codes)):
            for half in range(2):
                for g in range(kv_here):
                    scale = scales_ref[0, half, kind * KVH + tp * kv_here + g]
                    piece = codes[0, half * blk:(half + 1) * blk, g * HD:(g + 1) * HD]
                    gathered[kind][2 * ctx + half, :, g * HD:(g + 1) * HD] = (
                        piece.astype(jnp.float32) * scale
                    ).astype(jnp.bfloat16)

        def kv_copy(kind, k):
            return pltpu.make_async_remote_copy(
                src_ref=gathered[kind].at[here], dst_ref=gathered[kind].at[here],
                send_sem=kv_send.at[kind, k], recv_sem=kv_recv.at[kind, k],
                device_id=(pipe, lax.rem(ctx + k, cycle), tp), device_id_type=MESH,
            )

        for kind in range(2):
            for k in range(1, cycle):
                kv_copy(kind, k).start()

        @pl.loop(0, chunks)
        def _(c):
            o_copy(c).start()

        first = order_ref[2 * ctx]
        second = order_ref[2 * ctx + 1]
        first_hi = jnp.minimum(jnp.maximum(first - second, 0), 1)
        hi_block = jnp.maximum(first, second)
        lo_block = jnp.minimum(first, second)
        lo_count = lax.div(lo_block + 2, 2)

        float_hi, float_super = [], []
        for f in range(floats):
            is_hi = jnp.minimum(jnp.maximum(f + 2 - lo_count, 0), 1)
            float_hi.append(is_hi)
            float_super.append(jnp.clip(1 + f + is_hi * (sure - lo_count), 0, supers - 1))

        def choose(flag, one, other):
            return jnp.where(jnp.full(one.shape, flag, jnp.int32) > 0, one, other)

        def super_of(t):
            if t < sure:
                return t
            return 0 if t == sure else float_super[t - sure - 1]

        def pick(t, hi, lo):
            if t < sure:
                return hi
            if t == sure:
                return lo
            flag = float_hi[t - sure - 1]
            if hi.shape == ():
                return flag * hi + (1 - flag) * lo
            return choose(flag, hi, lo)

        for t in range(tasks):
            m = super_of(t)
            block = pick(t, hi_block, lo_block)
            key = lax.broadcasted_iota(jnp.int32, (2 * blk, width), 0)
            row = lax.broadcasted_iota(jnp.int32, (2 * blk, width), 1) % HD
            key_doc = jnp.where(key < blk, docs_ref[2 * m], docs_ref[2 * m + 1])
            seen = (key - row <= block * blk - m * (2 * blk)) & (key_doc == docs_ref[block])
            bias[t] = jnp.where(seen, 0.0, masked_floor)

        def stored_at(b):
            place = jnp.int32(0)
            for r in range(blocks):
                place = place + r * (1 - jnp.minimum(jnp.abs(order_ref[r] - b), 1))
            return jnp.minimum(place, blocks - 1)

        def sort_blocks(kind, seq):
            for k in range(1, cycle):
                kv_copy(kind, k).wait_recv()
            for b in range(blocks):
                piece = gathered[kind][stored_at(b)]
                for g in range(kv_here):
                    part = piece[:, g * HD:(g + 1) * HD]
                    lanes = pl.ds((b % 2) * blk, blk)
                    seq[g, b // 2, lanes, :] = part
                    if kind == 0:
                        turned = part.astype(jnp.float32).T.astype(jnp.bfloat16)
                        kt_seq[g, b // 2, :, lanes] = turned

        def stacked(buf, c):
            halves = []
            for half in range(2):
                piece = buf[c, half * blk:(half + 1) * blk, :]
                halves.append(jnp.concatenate(
                    [piece[:, h * HD:(h + 1) * HD] for h in range(HEADS_AT_ONCE)], axis=0
                ))
            return choose(first_hi, *halves), choose(first_hi, *halves[::-1])

        def combine(values, op, empty):
            hi, lo = None, values[sure]
            for t in range(sure):
                hi = values[t] if hi is None else op(hi, values[t])
            for f in range(floats):
                value = values[sure + 1 + f]
                hi = op(hi, choose(float_hi[f], value, empty))
                lo = op(lo, choose(1 - float_hi[f], value, empty))
            return hi, lo

        sort_blocks(0, k_seq)

        def find_probs(c):
            q_copy(c).wait()
            g = c // per_kv
            hi_query, lo_query = stacked(q_buf, c)
            scores, tops = [], []
            for t in range(tasks):
                query = pick(t, hi_query, lo_query)
                s = dot(k_seq[g, super_of(t)], query, NT) * inverse + bias[t]
                scores.append(s)
                tops.append(jnp.max(s, axis=0, keepdims=True))
            hi_top, lo_top = combine(tops, jnp.maximum, masked_floor)
            weights = [jnp.exp(scores[t] - pick(t, hi_top, lo_top)) for t in range(tasks)]
            sums = [jnp.sum(w, axis=0, keepdims=True) for w in weights]
            hi_sum, lo_sum = combine(sums, jnp.add, 0.0)
            hi_over, lo_over = 1.0 / hi_sum, 1.0 / lo_sum
            for t in range(tasks):
                probs[c, t] = (weights[t] * pick(t, hi_over, lo_over)).astype(jnp.bfloat16)

        @pl.loop(0, lead)
        def _(c):
            find_probs(c)

        sort_blocks(1, v_seq)

        def block_copy(g, k):
            flat, device = peer(k)
            return pltpu.make_async_remote_copy(
                src_ref=send_buf.at[g, flat], dst_ref=recv_buf.at[g, me],
                send_sem=g_send.at[g, k], recv_sem=g_recv.at[g, k],
                device_id=device, device_id_type=MESH,
            )

        for g in range(kv_here):
            dk_acc[...] = jnp.zeros_like(dk_acc)
            dv_acc[...] = jnp.zeros_like(dv_acc)

            @pl.loop(g * per_kv, (g + 1) * per_kv)
            def _(c):
                @pl.when(c + lead < chunks)
                def _():
                    find_probs(c + lead)

                o_copy(c).wait()
                z_copy(c).wait_recv()
                z_copy(c).wait_send()

                @pl.when(c + in_flight < chunks)
                def _():
                    z_copy(c + in_flight).start()

                dots = []
                for half in range(2):
                    here_rows = slice(half * blk, (half + 1) * blk)
                    both = do_buf[c, here_rows, :].astype(jnp.float32) * o_buf[
                        c, here_rows, :
                    ].astype(jnp.float32)
                    dots.append(jnp.concatenate([
                        jnp.sum(both[:, h * HD:(h + 1) * HD].T, axis=0, keepdims=True)
                        for h in range(HEADS_AT_ONCE)
                    ], axis=1))
                hi_dots, lo_dots = choose(first_hi, *dots), choose(first_hi, *dots[::-1])
                hi_query, lo_query = stacked(q_buf, c)
                hi_grad, lo_grad = stacked(do_buf, c)
                turned = []
                for t in range(tasks):
                    m = super_of(t)
                    query = pick(t, hi_query, lo_query)
                    grad = pick(t, hi_grad, lo_grad)
                    low = probs[c, t]
                    dp = dot(v_seq[g, m], grad, NT) - pick(t, hi_dots, lo_dots)
                    ds = (low.astype(jnp.float32) * dp).astype(jnp.bfloat16)
                    slot = t if t < sure else (0 if t == sure else supers + t - sure - 1)
                    dv_acc[2 * slot:2 * slot + 2] += dot(low, grad).reshape(2, blk, HD)
                    dk_acc[2 * slot:2 * slot + 2] += dot(ds, query).reshape(2, blk, HD)
                    turned.append(dot(kt_seq[g, m], ds))
                hi_turned, lo_turned = combine(turned, jnp.add, 0.0)
                top = choose(first_hi, hi_turned, lo_turned) * inverse
                low_half = choose(first_hi, lo_turned, hi_turned) * inverse
                for h in range(HEADS_AT_ONCE):
                    cols = slice(h * HD, (h + 1) * HD)
                    dq_buf[c, 0:blk, cols] = top[:, cols].T.astype(jnp.bfloat16)
                    dq_buf[c, blk:2 * blk, cols] = low_half[:, cols].T.astype(jnp.bfloat16)
                dq_copy(c).start()

            for kind, acc in ((0, dk_acc), (1, dv_acc)):
                for f in range(floats):
                    extra = acc[2 * (supers + f):2 * (supers + f) + 2]
                    for m in range(supers):
                        hit = 1 - jnp.minimum(jnp.abs(float_super[f] - m), 1)
                        acc[2 * m:2 * m + 2] += choose(hit, extra, 0.0)
                for r in range(blocks):
                    piece = acc[order_ref[r]]
                    send_buf[g, r, kind * blk:(kind + 1) * blk, :] = piece.astype(jnp.bfloat16)
            recv_buf[g, me] = send_buf[g, me]
            for k in range(1, peers):
                block_copy(g, k).start()

        for g in range(kv_here):
            for k in range(1, peers):
                block_copy(g, k).wait_recv()
            for t in range(tps):
                total = recv_buf[g, t].astype(jnp.float32)
                for d in range(1, cycle):
                    total = total + recv_buf[g, d * tps + t].astype(jnp.float32)
                cols = slice((t * kv_here + g) * HD, (t * kv_here + g + 1) * HD)
                dk_out[0, :, cols] = (total[:blk] * inverse).astype(jnp.bfloat16)
                dv_out[0, :, cols] = total[blk:].astype(jnp.bfloat16)

        @pl.loop(0, chunks)
        def _(c):
            dq_copy(c).wait()

        for kind in range(2):
            for k in range(1, cycle):
                kv_copy(kind, k).wait_send()
        for g in range(kv_here):
            for k in range(1, peers):
                block_copy(g, k).wait_send()

    bf16, f32 = jnp.bfloat16, jnp.float32
    scratch = [
        pltpu.VMEM((chunks, rows, width), bf16),
        pltpu.VMEM((chunks, rows, width), bf16),
        pltpu.VMEM((chunks, rows, width), bf16),
        pltpu.VMEM((chunks, rows, width), bf16),
        pltpu.VMEM((blocks, blk, kv_here * HD), bf16),
        pltpu.VMEM((blocks, blk, kv_here * HD), bf16),
        pltpu.VMEM((kv_here, supers, 2 * blk, HD), bf16),
        pltpu.VMEM((kv_here, supers, 2 * blk, HD), bf16),
        pltpu.VMEM((kv_here, supers, HD, 2 * blk), bf16),
        pltpu.VMEM((tasks, 2 * blk, width), f32),
        pltpu.VMEM((chunks, tasks, 2 * blk, width), bf16),
        pltpu.VMEM((2 * (supers + floats), blk, HD), f32),
        pltpu.VMEM((2 * (supers + floats), blk, HD), f32),
        pltpu.VMEM((kv_here, peers, 2 * blk, HD), bf16),
        pltpu.VMEM((kv_here, peers, 2 * blk, HD), bf16),
        pltpu.SemaphoreType.DMA((chunks,)),
        pltpu.SemaphoreType.DMA((chunks,)),
        pltpu.SemaphoreType.DMA((chunks,)),
        pltpu.SemaphoreType.DMA((chunks,)),
        pltpu.SemaphoreType.DMA((chunks,)),
        pltpu.SemaphoreType.DMA((2, cycle)),
        pltpu.SemaphoreType.DMA((2, cycle)),
        pltpu.SemaphoreType.DMA((kv_here, peers)),
        pltpu.SemaphoreType.DMA((kv_here, peers)),
    ]
    pairs = heads * tasks * 2 * blk * blk
    smem = pl.BlockSpec(memory_space=pltpu.SMEM)
    vmem = pl.BlockSpec(memory_space=pltpu.VMEM)
    hbm = pl.BlockSpec(memory_space=pl.ANY)
    return pl.pallas_call(
        kernel,
        out_shape=(
            jax.ShapeDtypeStruct((1, rows, heads * HD), bf16),
            jax.ShapeDtypeStruct((1, rows // tps, KVH * HD), bf16),
            jax.ShapeDtypeStruct((1, rows // tps, KVH * HD), bf16),
        ),
        in_specs=[smem, smem, smem, vmem, vmem, hbm, hbm, hbm],
        out_specs=(hbm, vmem, vmem),
        scratch_shapes=scratch,
        compiler_params=pltpu.CompilerParams(
            collective_id=0, has_side_effects=True, vmem_limit_bytes=56 << 20
        ),
        cost_estimate=pl.CostEstimate(
            flops=5 * 2 * HD * pairs, bytes_accessed=5 * rows * heads * HD * 2,
            transcendentals=pairs,
        ),
    )


def hand_over(*arrays):
    pieces = 8

    def kernel(*refs):
        sources, targets, sems = refs[:len(arrays)], refs[len(arrays):-1], refs[-1]
        copies = []
        for source, target in zip(sources, targets):
            count = pieces if source is sources[0] else 1
            step = source.shape[1] // count
            for i in range(count):
                part = pl.ds(i * step, step)
                copies.append(pltpu.make_async_copy(
                    source.at[0, part], target.at[0, part], sems.at[len(copies)]
                ))
        for copy in copies:
            copy.start()
        for copy in copies:
            copy.wait()

    hbm = pl.BlockSpec(memory_space=pl.ANY)
    return pl.pallas_call(
        kernel,
        out_shape=tuple(jax.ShapeDtypeStruct(a.shape, a.dtype) for a in arrays),
        in_specs=[hbm] * len(arrays),
        out_specs=(hbm,) * len(arrays),
        scratch_shapes=[pltpu.SemaphoreType.DMA((pieces + len(arrays) - 1,))],
        compiler_params=pltpu.CompilerParams(vmem_limit_bytes=56 << 20),
    )(*arrays)


def solution(mesh):
    sizes = (mesh.shape["pipe"], mesh.shape["ctx"], mesh.shape["tp"])

    def on_device(
        queries, key_codes, value_codes, kv_scales, saved_out, section_grads, block_order, block_docs
    ):
        call = make_kernel(
            sizes, queries.shape[1], queries.shape[2] // HD, key_codes.shape[2] // HD,
            block_order.shape[0],
        )
        return hand_over(*call(
            block_order, block_docs, kv_scales, key_codes, value_codes, queries, saved_out,
            section_grads,
        ))

    in_specs = (
        P("pipe", "ctx", "tp"),
        P("pipe", "ctx", "tp"),
        P("pipe", "ctx", "tp"),
        P("pipe", "ctx", None),
        P("pipe", "ctx", "tp"),
        P("pipe", "ctx", "tp"),
        P(),
        P(),
    )
    out_specs = (
        P("pipe", "ctx", "tp"),
        P("pipe", ("ctx", "tp"), None),
        P("pipe", ("ctx", "tp"), None),
    )
    return jax.shard_map(
        on_device, mesh=mesh, in_specs=in_specs, out_specs=out_specs, check_vma=False
    )
```

```python
import jax
import jax.numpy as jnp
from jax import lax
from jax.experimental import pallas as pl
from jax.experimental.pallas import tpu as pltpu
from jax.sharding import PartitionSpec as P

HQ = 64
KVH = 4
HD = 128
HEADS_AT_ONCE = 2
LEAD = 1

masked_floor = -1e30
MESH = pl.DeviceIdType.MESH
NT = (((1,), (1,)), ((), ()))
LOG2_E = 1.4426950408889634
NN = (((1,), (0,)), ((), ()))


def dot(a, b, dims=NN):
    return lax.dot_general(a, b, dims, preferred_element_type=jnp.float32)


def make_kernel(sizes, rows, heads, kv_here, blocks):
    pipes, cycle, tps = sizes
    blk = rows // 2
    width = HEADS_AT_ONCE * HD
    chunks = heads // HEADS_AT_ONCE
    per_kv = chunks // kv_here
    lead = LEAD
    supers = blocks // 2
    sure = blocks // 4 + 1
    floats = supers - sure
    tasks = sure + 1 + floats
    peers = cycle * tps
    inverse = HD ** (-0.5)

    def kernel(
        order_ref, docs_ref, scales_ref, key_codes, value_codes, queries, saved, grads,
        dq_out, dk_out, dv_out,
        q_buf, o_buf, do_buf, dq_buf, k_all, v_all, k_seq, v_seq, kt_seq, bias, probs,
        dk_acc, dv_acc, send_buf, recv_buf,
        q_sem, o_sem, dq_sem, z_send, z_recv, kv_send, kv_recv, g_send, g_recv,
    ):
        pipe = lax.axis_index("pipe")
        ctx = lax.axis_index("ctx")
        tp = lax.axis_index("tp")
        me = ctx * tps + tp
        ahead = lax.rem(pipe + 1, pipes)
        behind = lax.rem(pipe + pipes - 1, pipes)

        def peer(k):
            flat = lax.rem(me + k, peers)
            return flat, (pipe, flat // tps, lax.rem(flat, tps))

        barrier = pltpu.get_barrier_semaphore()
        for where in (ahead, behind):
            pl.semaphore_signal(barrier, inc=1, device_id=(where, ctx, tp), device_id_type=MESH)
        for k in range(1, peers):
            pl.semaphore_signal(barrier, inc=1, device_id=peer(k)[1], device_id_type=MESH)
        pl.semaphore_wait(barrier, peers + 1)

        def columns(ref, c):
            return ref.at[0, :, pl.ds(pl.multiple_of(c * width, width), width)]

        def z_copy(c):
            return pltpu.make_async_remote_copy(
                src_ref=columns(grads, c), dst_ref=do_buf.at[c],
                send_sem=z_send.at[c], recv_sem=z_recv.at[c],
                device_id=(behind, ctx, tp), device_id_type=MESH,
            )

        def q_copy(c):
            return pltpu.make_async_copy(columns(queries, c), q_buf.at[c], q_sem.at[c])

        def o_copy(c):
            return pltpu.make_async_copy(columns(saved, c), o_buf.at[c], o_sem.at[c])

        def dq_copy(c):
            return pltpu.make_async_copy(dq_buf.at[c], columns(dq_out, c), dq_sem.at[c])

        @pl.loop(0, chunks)
        def _(c):
            z_copy(c).start()

        @pl.loop(0, chunks)
        def _(c):
            q_copy(c).start()

        here = pl.ds(2 * ctx, 2)
        gathered = (k_all, v_all)
        for kind, codes in ((0, key_codes), (1, value_codes)):
            for half in range(2):
                for g in range(kv_here):
                    scale = scales_ref[0, half, kind * KVH + tp * kv_here + g]
                    piece = codes[0, half * blk:(half + 1) * blk, g * HD:(g + 1) * HD]
                    gathered[kind][2 * ctx + half, :, g * HD:(g + 1) * HD] = (
                        piece.astype(jnp.float32) * scale
                    ).astype(jnp.bfloat16)

        def kv_copy(kind, k):
            return pltpu.make_async_remote_copy(
                src_ref=gathered[kind].at[here], dst_ref=gathered[kind].at[here],
                send_sem=kv_send.at[kind, k], recv_sem=kv_recv.at[kind, k],
                device_id=(pipe, lax.rem(ctx + k, cycle), tp), device_id_type=MESH,
            )

        for kind in range(2):
            for k in range(1, cycle):
                kv_copy(kind, k).start()

        @pl.loop(0, chunks)
        def _(c):
            o_copy(c).start()

        first = order_ref[2 * ctx]
        second = order_ref[2 * ctx + 1]
        first_hi = jnp.minimum(jnp.maximum(first - second, 0), 1)
        hi_block = jnp.maximum(first, second)
        lo_block = jnp.minimum(first, second)
        lo_count = lax.div(lo_block + 2, 2)

        float_hi, float_super = [], []
        for f in range(floats):
            is_hi = jnp.minimum(jnp.maximum(f + 2 - lo_count, 0), 1)
            float_hi.append(is_hi)
            float_super.append(jnp.clip(1 + f + is_hi * (sure - lo_count), 0, supers - 1))

        def choose(flag, one, other):
            return jnp.where(jnp.full(one.shape, flag, jnp.int32) > 0, one, other)

        def super_of(t):
            if t < sure:
                return t
            return 0 if t == sure else float_super[t - sure - 1]

        groups = [(0, sure), (sure, sure + 1)] + [(t, t + 1) for t in range(sure + 1, tasks)]

        def of_group(ref, g, u):
            if u == 0:
                return ref[g, 0:sure].reshape(sure * 2 * blk, HD)
            return ref[g, super_of(groups[u][0])]

        def turned_of_group(g, u):
            if u == 0:
                return jnp.concatenate([kt_seq[g, m] for m in range(sure)], axis=1)
            return kt_seq[g, super_of(groups[u][0])]

        def pick(u, hi, lo):
            if u < 2:
                return lo if u else hi
            flag = float_hi[u - 2]
            if hi.shape == ():
                return flag * hi + (1 - flag) * lo
            return choose(flag, hi, lo)

        for t in range(tasks):
            m = super_of(t)
            block = pick(max(t - sure + 1, 0), hi_block, lo_block)
            key = lax.broadcasted_iota(jnp.int32, (2 * blk, width), 0)
            row = lax.broadcasted_iota(jnp.int32, (2 * blk, width), 1) % HD
            key_doc = jnp.where(key < blk, docs_ref[2 * m], docs_ref[2 * m + 1])
            seen = (key - row <= block * blk - m * (2 * blk)) & (key_doc == docs_ref[block])
            bias[t * 2 * blk:(t + 1) * 2 * blk] = jnp.where(seen, 0.0, masked_floor)

        def stored_at(b):
            place = jnp.int32(0)
            for r in range(blocks):
                place = place + r * (1 - jnp.minimum(jnp.abs(order_ref[r] - b), 1))
            return jnp.minimum(place, blocks - 1)

        def sort_blocks(kind, seq):
            for k in range(1, cycle):
                kv_copy(kind, k).wait_recv()
            for b in range(blocks):
                piece = gathered[kind][stored_at(b)]
                for g in range(kv_here):
                    part = piece[:, g * HD:(g + 1) * HD]
                    lanes = pl.ds((b % 2) * blk, blk)
                    seq[g, b // 2, lanes, :] = part
                    if kind == 0:
                        turned = part.astype(jnp.float32).T.astype(jnp.bfloat16)
                        kt_seq[g, b // 2, :, lanes] = turned

        def stacked(buf, c):
            halves = []
            for half in range(2):
                piece = buf[c, half * blk:(half + 1) * blk, :]
                halves.append(jnp.concatenate(
                    [piece[:, h * HD:(h + 1) * HD] for h in range(HEADS_AT_ONCE)], axis=0
                ))
            return choose(first_hi, *halves), choose(first_hi, *halves[::-1])

        def combine(values, op, empty):
            hi, lo = values[0], values[1]
            for f in range(floats):
                value = values[2 + f]
                hi = op(hi, choose(float_hi[f], value, empty))
                lo = op(lo, choose(1 - float_hi[f], value, empty))
            return hi, lo

        sort_blocks(0, k_seq)

        def find_probs(c):
            g = c // per_kv
            hi_query, lo_query = stacked(q_buf, c)
            scores, tops = [], []
            for u, (begin, end) in enumerate(groups):
                query = pick(u, hi_query, lo_query)
                part = slice(begin * 2 * blk, end * 2 * blk)
                s = dot(of_group(k_seq, g, u), query, NT) * (inverse * LOG2_E) + bias[part]
                scores.append(s)
                tops.append(jnp.max(s, axis=0, keepdims=True))
            hi_top, lo_top = combine(tops, jnp.maximum, masked_floor)
            weights = [jnp.exp2(s - pick(u, hi_top, lo_top)) for u, s in enumerate(scores)]
            sums = [jnp.sum(w, axis=0, keepdims=True) for w in weights]
            hi_sum, lo_sum = combine(sums, jnp.add, 0.0)
            hi_over, lo_over = 1.0 / hi_sum, 1.0 / lo_sum
            for u, (begin, end) in enumerate(groups):
                part = slice(begin * 2 * blk, end * 2 * blk)
                probs[c, part] = (weights[u] * pick(u, hi_over, lo_over)).astype(jnp.bfloat16)

        @pl.loop(0, lead)
        def _(c):
            q_copy(c).wait()
            find_probs(c)

        sort_blocks(1, v_seq)

        def block_copy(g, k):
            flat, device = peer(k)
            return pltpu.make_async_remote_copy(
                src_ref=send_buf.at[g, flat], dst_ref=recv_buf.at[g, me],
                send_sem=g_send.at[g, k], recv_sem=g_recv.at[g, k],
                device_id=device, device_id_type=MESH,
            )

        for g in range(kv_here):
            dk_acc[...] = jnp.zeros_like(dk_acc)
            dv_acc[...] = jnp.zeros_like(dv_acc)

            def backward(c, more):
                o_copy(c).wait()
                z_copy(c).wait_recv()
                if more:
                    q_copy(c + lead).wait()
                    find_probs(c + lead)
                dots = []
                for half in range(2):
                    here_rows = slice(half * blk, (half + 1) * blk)
                    both = do_buf[c, here_rows, :].astype(jnp.float32) * o_buf[
                        c, here_rows, :
                    ].astype(jnp.float32)
                    dots.append(jnp.concatenate([
                        jnp.sum(both[:, h * HD:(h + 1) * HD].T, axis=0, keepdims=True)
                        for h in range(HEADS_AT_ONCE)
                    ], axis=1))
                hi_dots, lo_dots = choose(first_hi, *dots), choose(first_hi, *dots[::-1])
                hi_query, lo_query = stacked(q_buf, c)
                hi_grad, lo_grad = stacked(do_buf, c)
                turned = []
                for u, (begin, end) in enumerate(groups):
                    query = pick(u, hi_query, lo_query)
                    grad = pick(u, hi_grad, lo_grad)
                    low = probs[c, begin * 2 * blk:end * 2 * blk]
                    dp = dot(of_group(v_seq, g, u), grad, NT) - pick(u, hi_dots, lo_dots)
                    ds = (low.astype(jnp.float32) * dp).astype(jnp.bfloat16)
                    first_slot = 0 if u < 2 else supers + u - 2
                    slots = slice(2 * first_slot, 2 * (first_slot + end - begin))
                    dv_acc[slots] += dot(low, grad).reshape(2 * (end - begin), blk, HD)
                    dk_acc[slots] += dot(ds, query).reshape(2 * (end - begin), blk, HD)
                    turned.append(dot(turned_of_group(g, u), ds))
                hi_turned, lo_turned = combine(turned, jnp.add, 0.0)
                top = choose(first_hi, hi_turned, lo_turned) * inverse
                low_half = choose(first_hi, lo_turned, hi_turned) * inverse
                for h in range(HEADS_AT_ONCE):
                    cols = slice(h * HD, (h + 1) * HD)
                    dq_buf[c, 0:blk, cols] = top[:, cols].T.astype(jnp.bfloat16)
                    dq_buf[c, blk:2 * blk, cols] = low_half[:, cols].T.astype(jnp.bfloat16)
                dq_copy(c).start()

            stop = min((g + 1) * per_kv, chunks - lead)

            @pl.loop(g * per_kv, stop)
            def _(c):
                backward(c, True)

            if stop < (g + 1) * per_kv:
                @pl.loop(stop, (g + 1) * per_kv)
                def _(c):
                    backward(c, False)

            for kind, acc in ((0, dk_acc), (1, dv_acc)):
                for f in range(floats):
                    extra = acc[2 * (supers + f):2 * (supers + f) + 2]
                    for m in range(supers):
                        hit = 1 - jnp.minimum(jnp.abs(float_super[f] - m), 1)
                        acc[2 * m:2 * m + 2] += choose(hit, extra, 0.0)
                for r in range(blocks):
                    piece = acc[order_ref[r]]
                    send_buf[g, r, kind * blk:(kind + 1) * blk, :] = piece.astype(jnp.bfloat16)
            recv_buf[g, me] = send_buf[g, me]
            for k in range(1, peers):
                block_copy(g, k).start()

        for g in range(kv_here):
            for k in range(1, peers):
                block_copy(g, k).wait_recv()
            for t in range(tps):
                total = recv_buf[g, t].astype(jnp.float32)
                for d in range(1, cycle):
                    total = total + recv_buf[g, d * tps + t].astype(jnp.float32)
                cols = slice((t * kv_here + g) * HD, (t * kv_here + g + 1) * HD)
                dk_out[0, :, cols] = (total[:blk] * inverse).astype(jnp.bfloat16)
                dv_out[0, :, cols] = total[blk:].astype(jnp.bfloat16)

        @pl.loop(0, chunks)
        def _(c):
            z_copy(c).wait_send()
            dq_copy(c).wait()

        for kind in range(2):
            for k in range(1, cycle):
                kv_copy(kind, k).wait_send()
        for g in range(kv_here):
            for k in range(1, peers):
                block_copy(g, k).wait_send()

    bf16, f32 = jnp.bfloat16, jnp.float32
    scratch = [
        pltpu.VMEM((chunks, rows, width), bf16),
        pltpu.VMEM((chunks, rows, width), bf16),
        pltpu.VMEM((chunks, rows, width), bf16),
        pltpu.VMEM((chunks, rows, width), bf16),
        pltpu.VMEM((blocks, blk, kv_here * HD), bf16),
        pltpu.VMEM((blocks, blk, kv_here * HD), bf16),
        pltpu.VMEM((kv_here, supers, 2 * blk, HD), bf16),
        pltpu.VMEM((kv_here, supers, 2 * blk, HD), bf16),
        pltpu.VMEM((kv_here, supers, HD, 2 * blk), bf16),
        pltpu.VMEM((tasks * 2 * blk, width), f32),
        pltpu.VMEM((chunks, tasks * 2 * blk, width), bf16),
        pltpu.VMEM((2 * (supers + floats), blk, HD), f32),
        pltpu.VMEM((2 * (supers + floats), blk, HD), f32),
        pltpu.VMEM((kv_here, peers, 2 * blk, HD), bf16),
        pltpu.VMEM((kv_here, peers, 2 * blk, HD), bf16),
        pltpu.SemaphoreType.DMA((chunks,)),
        pltpu.SemaphoreType.DMA((chunks,)),
        pltpu.SemaphoreType.DMA((chunks,)),
        pltpu.SemaphoreType.DMA((chunks,)),
        pltpu.SemaphoreType.DMA((chunks,)),
        pltpu.SemaphoreType.DMA((2, cycle)),
        pltpu.SemaphoreType.DMA((2, cycle)),
        pltpu.SemaphoreType.DMA((kv_here, peers)),
        pltpu.SemaphoreType.DMA((kv_here, peers)),
    ]
    pairs = heads * tasks * 2 * blk * blk
    smem = pl.BlockSpec(memory_space=pltpu.SMEM)
    vmem = pl.BlockSpec(memory_space=pltpu.VMEM)
    hbm = pl.BlockSpec(memory_space=pl.ANY)
    return pl.pallas_call(
        kernel,
        out_shape=(
            jax.ShapeDtypeStruct((1, rows, heads * HD), bf16),
            jax.ShapeDtypeStruct((1, rows // tps, KVH * HD), bf16),
            jax.ShapeDtypeStruct((1, rows // tps, KVH * HD), bf16),
        ),
        in_specs=[smem, smem, smem, vmem, vmem, hbm, hbm, hbm],
        out_specs=(hbm, vmem, vmem),
        scratch_shapes=scratch,
        compiler_params=pltpu.CompilerParams(
            collective_id=0, has_side_effects=True, vmem_limit_bytes=56 << 20
        ),
        cost_estimate=pl.CostEstimate(
            flops=5 * 2 * HD * pairs, bytes_accessed=5 * rows * heads * HD * 2,
            transcendentals=pairs,
        ),
    )


def hand_over(*arrays):
    pieces = 8

    count = len(arrays)

    def kernel(*refs):
        sources, targets, held = refs[:count], refs[count:2 * count], refs[2 * count:3 * count]
        in_sems, out_sems = refs[3 * count:]
        inward, outward = [], []
        for source, target, middle in zip(sources, targets, held):
            parts = pieces if source is sources[0] else 1
            step = source.shape[1] // parts
            for i in range(parts):
                part, at = pl.ds(i * step, step), len(inward)
                inward.append(pltpu.make_async_copy(
                    source.at[0, part], middle.at[part], in_sems.at[at]
                ))
                outward.append(pltpu.make_async_copy(
                    middle.at[part], target.at[0, part], out_sems.at[at]
                ))
        for copy in inward:
            copy.start()
        for copy, onward in zip(inward, outward):
            copy.wait()
            onward.start()
        for copy in outward:
            copy.wait()

    hbm = pl.BlockSpec(memory_space=pl.ANY)
    return pl.pallas_call(
        kernel,
        out_shape=tuple(jax.ShapeDtypeStruct(a.shape, a.dtype) for a in arrays),
        in_specs=[hbm] * len(arrays),
        out_specs=(hbm,) * len(arrays),
        scratch_shapes=[pltpu.VMEM(a.shape[1:], a.dtype) for a in arrays]
        + [pltpu.SemaphoreType.DMA((pieces + count - 1,))] * 2,
        compiler_params=pltpu.CompilerParams(vmem_limit_bytes=56 << 20),
    )(*arrays)


def solution(mesh):
    sizes = (mesh.shape["pipe"], mesh.shape["ctx"], mesh.shape["tp"])

    def on_device(
        queries, key_codes, value_codes, kv_scales, saved_out, section_grads, block_order, block_docs
    ):
        call = make_kernel(
            sizes, queries.shape[1], queries.shape[2] // HD, key_codes.shape[2] // HD,
            block_order.shape[0],
        )
        return hand_over(*call(
            block_order, block_docs, kv_scales, key_codes, value_codes, queries, saved_out,
            section_grads,
        ))

    in_specs = (
        P("pipe", "ctx", "tp"),
        P("pipe", "ctx", "tp"),
        P("pipe", "ctx", "tp"),
        P("pipe", "ctx", None),
        P("pipe", "ctx", "tp"),
        P("pipe", "ctx", "tp"),
        P(),
        P(),
    )
    out_specs = (
        P("pipe", "ctx", "tp"),
        P("pipe", ("ctx", "tp"), None),
        P("pipe", ("ctx", "tp"), None),
    )
    return jax.shard_map(
        on_device, mesh=mesh, in_specs=in_specs, out_specs=out_specs, check_vma=False
    )
```

```python
import jax
import jax.numpy as jnp
from jax import lax
from jax.experimental import pallas as pl
from jax.experimental.pallas import tpu as pltpu
from jax.sharding import PartitionSpec as P

HQ = 64
KVH = 4
HD = 128
HEADS_AT_ONCE = 2
LEAD = 1

masked_floor = -1e30
MESH = pl.DeviceIdType.MESH
NT = (((1,), (1,)), ((), ()))
LOG2_E = 1.4426950408889634
NN = (((1,), (0,)), ((), ()))


def dot(a, b, dims=NN):
    return lax.dot_general(a, b, dims, preferred_element_type=jnp.float32)


def make_kernel(sizes, rows, heads, kv_here, blocks):
    pipes, cycle, tps = sizes
    blk = rows // 2
    width = HEADS_AT_ONCE * HD
    chunks = heads // HEADS_AT_ONCE
    per_kv = chunks // kv_here
    lead = LEAD
    supers = blocks // 2
    sure = blocks // 4 + 1
    floats = supers - sure
    tasks = sure + 1 + floats
    peers = cycle * tps
    inverse = HD ** (-0.5)

    def kernel(
        order_ref, docs_ref, scales_ref, key_codes, value_codes, queries, saved, grads,
        dq_out, dk_out, dv_out,
        q_buf, o_buf, do_buf, dq_buf, k_all, v_all, k_seq, v_seq, kt_seq, bias, probs,
        dk_acc, dv_acc, send_buf, recv_buf,
        q_sem, o_sem, dq_sem, z_send, z_recv, kv_send, kv_recv, g_send, g_recv,
    ):
        pipe = lax.axis_index("pipe")
        ctx = lax.axis_index("ctx")
        tp = lax.axis_index("tp")
        me = ctx * tps + tp
        ahead = lax.rem(pipe + 1, pipes)
        behind = lax.rem(pipe + pipes - 1, pipes)

        def peer(k):
            flat = lax.rem(me + k, peers)
            return flat, (pipe, flat // tps, lax.rem(flat, tps))

        barrier = pltpu.get_barrier_semaphore()
        for where in (ahead, behind):
            pl.semaphore_signal(barrier, inc=1, device_id=(where, ctx, tp), device_id_type=MESH)
        for k in range(1, peers):
            pl.semaphore_signal(barrier, inc=1, device_id=peer(k)[1], device_id_type=MESH)
        pl.semaphore_wait(barrier, peers + 1)

        def columns(ref, c):
            return ref.at[0, :, pl.ds(pl.multiple_of(c * width, width), width)]

        def z_copy(c):
            return pltpu.make_async_remote_copy(
                src_ref=columns(grads, c), dst_ref=do_buf.at[c],
                send_sem=z_send.at[c], recv_sem=z_recv.at[c],
                device_id=(behind, ctx, tp), device_id_type=MESH,
            )

        def q_copy(c):
            return pltpu.make_async_copy(columns(queries, c), q_buf.at[c], q_sem.at[c])

        def o_copy(c):
            return pltpu.make_async_copy(columns(saved, c), o_buf.at[c], o_sem.at[c])

        def dq_copy(c):
            return pltpu.make_async_copy(dq_buf.at[c], columns(dq_out, c), dq_sem.at[c])

        @pl.loop(0, chunks)
        def _(c):
            z_copy(c).start()

        @pl.loop(0, chunks)
        def _(c):
            q_copy(c).start()

        here = pl.ds(2 * ctx, 2)
        gathered = (k_all, v_all)
        for kind, codes in ((0, key_codes), (1, value_codes)):
            for half in range(2):
                for g in range(kv_here):
                    scale = scales_ref[0, half, kind * KVH + tp * kv_here + g]
                    piece = codes[0, half * blk:(half + 1) * blk, g * HD:(g + 1) * HD]
                    gathered[kind][2 * ctx + half, :, g * HD:(g + 1) * HD] = (
                        piece.astype(jnp.float32) * scale
                    ).astype(jnp.bfloat16)

        def kv_copy(kind, k):
            return pltpu.make_async_remote_copy(
                src_ref=gathered[kind].at[here], dst_ref=gathered[kind].at[here],
                send_sem=kv_send.at[kind, k], recv_sem=kv_recv.at[kind, k],
                device_id=(pipe, lax.rem(ctx + k, cycle), tp), device_id_type=MESH,
            )

        for kind in range(2):
            for k in range(1, cycle):
                kv_copy(kind, k).start()

        @pl.loop(0, chunks)
        def _(c):
            o_copy(c).start()

        first = order_ref[2 * ctx]
        second = order_ref[2 * ctx + 1]
        first_hi = jnp.minimum(jnp.maximum(first - second, 0), 1)
        hi_block = jnp.maximum(first, second)
        lo_block = jnp.minimum(first, second)
        lo_count = lax.div(lo_block + 2, 2)

        float_hi, float_super = [], []
        for f in range(floats):
            is_hi = jnp.minimum(jnp.maximum(f + 2 - lo_count, 0), 1)
            float_hi.append(is_hi)
            float_super.append(jnp.clip(1 + f + is_hi * (sure - lo_count), 0, supers - 1))

        def choose(flag, one, other):
            return jnp.where(jnp.full(one.shape, flag, jnp.int32) > 0, one, other)

        def super_of(t):
            if t < sure:
                return t
            return 0 if t == sure else float_super[t - sure - 1]

        groups = [(0, sure), (sure, sure + 1)] + [(t, t + 1) for t in range(sure + 1, tasks)]

        def of_group(ref, g, u):
            if u == 0:
                return ref[g, 0:sure].reshape(sure * 2 * blk, HD)
            return ref[g, super_of(groups[u][0])]

        def turned_of_group(g, u):
            if u == 0:
                return jnp.concatenate([kt_seq[g, m] for m in range(sure)], axis=1)
            return kt_seq[g, super_of(groups[u][0])]

        def pick(u, hi, lo):
            if u < 2:
                return lo if u else hi
            flag = float_hi[u - 2]
            if hi.shape == ():
                return flag * hi + (1 - flag) * lo
            return choose(flag, hi, lo)

        for t in range(tasks):
            m = super_of(t)
            block = pick(max(t - sure + 1, 0), hi_block, lo_block)
            key = lax.broadcasted_iota(jnp.int32, (2 * blk, width), 0)
            row = lax.broadcasted_iota(jnp.int32, (2 * blk, width), 1) % HD
            key_doc = jnp.where(key < blk, docs_ref[2 * m], docs_ref[2 * m + 1])
            seen = (key - row <= block * blk - m * (2 * blk)) & (key_doc == docs_ref[block])
            bias[t * 2 * blk:(t + 1) * 2 * blk] = jnp.where(seen, 0.0, masked_floor)

        def stored_at(b):
            place = jnp.int32(0)
            for r in range(blocks):
                place = place + r * (1 - jnp.minimum(jnp.abs(order_ref[r] - b), 1))
            return jnp.minimum(place, blocks - 1)

        def sort_blocks(kind, seq):
            for k in range(1, cycle):
                kv_copy(kind, k).wait_recv()
            for b in range(blocks):
                piece = gathered[kind][stored_at(b)]
                for g in range(kv_here):
                    part = piece[:, g * HD:(g + 1) * HD]
                    lanes = pl.ds((b % 2) * blk, blk)
                    seq[g, b // 2, lanes, :] = part
                    if kind == 0:
                        turned = part.astype(jnp.float32).T.astype(jnp.bfloat16)
                        kt_seq[g, b // 2, :, lanes] = turned

        def stacked(buf, c):
            halves = []
            for half in range(2):
                piece = buf[c, half * blk:(half + 1) * blk, :]
                halves.append(jnp.concatenate(
                    [piece[:, h * HD:(h + 1) * HD] for h in range(HEADS_AT_ONCE)], axis=0
                ))
            return choose(first_hi, *halves), choose(first_hi, *halves[::-1])

        def combine(values, op, empty):
            hi, lo = values[0], values[1]
            for f in range(floats):
                value = values[2 + f]
                hi = op(hi, choose(float_hi[f], value, empty))
                lo = op(lo, choose(1 - float_hi[f], value, empty))
            return hi, lo

        sort_blocks(0, k_seq)

        def find_probs(c):
            g = c // per_kv
            hi_query, lo_query = stacked(q_buf, c)
            scores, tops = [], []
            for u, (begin, end) in enumerate(groups):
                query = pick(u, hi_query, lo_query)
                part = slice(begin * 2 * blk, end * 2 * blk)
                s = dot(of_group(k_seq, g, u), query, NT) * (inverse * LOG2_E) + bias[part]
                scores.append(s)
                tops.append(jnp.max(s, axis=0, keepdims=True))
            hi_top, lo_top = combine(tops, jnp.maximum, masked_floor)
            weights = [jnp.exp2(s - pick(u, hi_top, lo_top)) for u, s in enumerate(scores)]
            sums = [jnp.sum(w, axis=0, keepdims=True) for w in weights]
            hi_sum, lo_sum = combine(sums, jnp.add, 0.0)
            hi_over, lo_over = 1.0 / hi_sum, 1.0 / lo_sum
            for u, (begin, end) in enumerate(groups):
                part = slice(begin * 2 * blk, end * 2 * blk)
                probs[c, part] = (weights[u] * pick(u, hi_over, lo_over)).astype(jnp.bfloat16)

        @pl.loop(0, lead)
        def _(c):
            q_copy(c).wait()
            find_probs(c)

        sort_blocks(1, v_seq)

        def block_copy(g, k):
            flat, device = peer(k)
            return pltpu.make_async_remote_copy(
                src_ref=send_buf.at[g, flat], dst_ref=recv_buf.at[g, me],
                send_sem=g_send.at[g, k], recv_sem=g_recv.at[g, k],
                device_id=device, device_id_type=MESH,
            )

        for g in range(kv_here):
            dk_acc[...] = jnp.zeros_like(dk_acc)
            dv_acc[...] = jnp.zeros_like(dv_acc)

            def backward(c, more):
                o_copy(c).wait()
                z_copy(c).wait_recv()
                if more:
                    q_copy(c + lead).wait()
                    find_probs(c + lead)
                dots = []
                for half in range(2):
                    here_rows = slice(half * blk, (half + 1) * blk)
                    both = do_buf[c, here_rows, :].astype(jnp.float32) * o_buf[
                        c, here_rows, :
                    ].astype(jnp.float32)
                    dots.append(jnp.concatenate([
                        jnp.sum(both[:, h * HD:(h + 1) * HD].T, axis=0, keepdims=True)
                        for h in range(HEADS_AT_ONCE)
                    ], axis=1))
                hi_dots, lo_dots = choose(first_hi, *dots), choose(first_hi, *dots[::-1])
                hi_query, lo_query = stacked(q_buf, c)
                hi_grad, lo_grad = stacked(do_buf, c)
                changes = []
                for u, (begin, end) in enumerate(groups):
                    query = pick(u, hi_query, lo_query)
                    grad = pick(u, hi_grad, lo_grad)
                    low = probs[c, begin * 2 * blk:end * 2 * blk]
                    dp = dot(of_group(v_seq, g, u), grad, NT) - pick(u, hi_dots, lo_dots)
                    ds = (low.astype(jnp.float32) * dp).astype(jnp.bfloat16)
                    first_slot = 0 if u < 2 else supers + u - 2
                    slots = slice(2 * first_slot, 2 * (first_slot + end - begin))
                    dv_acc[slots] += dot(low, grad).reshape(2 * (end - begin), blk, HD)
                    dk_acc[slots] += dot(ds, query).reshape(2 * (end - begin), blk, HD)
                    changes.append(ds)
                if more:
                    finish(c, changes)
                return changes

            def finish(c, changes):
                turned = [dot(turned_of_group(g, u), ds) for u, ds in enumerate(changes)]
                hi_turned, lo_turned = combine(turned, jnp.add, 0.0)
                top = choose(first_hi, hi_turned, lo_turned) * inverse
                low_half = choose(first_hi, lo_turned, hi_turned) * inverse
                for h in range(HEADS_AT_ONCE):
                    cols = slice(h * HD, (h + 1) * HD)
                    dq_buf[c, 0:blk, cols] = top[:, cols].T.astype(jnp.bfloat16)
                    dq_buf[c, blk:2 * blk, cols] = low_half[:, cols].T.astype(jnp.bfloat16)
                dq_copy(c).start()

            stop = min((g + 1) * per_kv, chunks - lead)

            @pl.loop(g * per_kv, stop)
            def _(c):
                backward(c, True)

            last = chunks - 1 if stop < (g + 1) * per_kv else None
            if last is not None:
                changes = backward(last, False)

            for kind, acc in ((0, dk_acc), (1, dv_acc)):
                for f in range(floats):
                    extra = acc[2 * (supers + f):2 * (supers + f) + 2]
                    for m in range(supers):
                        hit = 1 - jnp.minimum(jnp.abs(float_super[f] - m), 1)
                        acc[2 * m:2 * m + 2] += choose(hit, extra, 0.0)

            def prepare(r):
                b = order_ref[r]
                send_buf[g, r, 0:blk, :] = dk_acc[b].astype(jnp.bfloat16)
                send_buf[g, r, blk:2 * blk, :] = dv_acc[b].astype(jnp.bfloat16)

            for k in range(1, peers):
                prepare(peer(k)[0])
                block_copy(g, k).start()
            prepare(me)
            recv_buf[g, me] = send_buf[g, me]
            if last is not None:
                finish(last, changes)

        for g in range(kv_here):
            for k in range(1, peers):
                block_copy(g, k).wait_recv()
            for t in range(tps):
                total = recv_buf[g, t].astype(jnp.float32)
                for d in range(1, cycle):
                    total = total + recv_buf[g, d * tps + t].astype(jnp.float32)
                cols = slice((t * kv_here + g) * HD, (t * kv_here + g + 1) * HD)
                dk_out[0, :, cols] = (total[:blk] * inverse).astype(jnp.bfloat16)
                dv_out[0, :, cols] = total[blk:].astype(jnp.bfloat16)

        @pl.loop(0, chunks)
        def _(c):
            z_copy(c).wait_send()
            dq_copy(c).wait()

        for kind in range(2):
            for k in range(1, cycle):
                kv_copy(kind, k).wait_send()
        for g in range(kv_here):
            for k in range(1, peers):
                block_copy(g, k).wait_send()

    bf16, f32 = jnp.bfloat16, jnp.float32
    scratch = [
        pltpu.VMEM((chunks, rows, width), bf16),
        pltpu.VMEM((chunks, rows, width), bf16),
        pltpu.VMEM((chunks, rows, width), bf16),
        pltpu.VMEM((chunks, rows, width), bf16),
        pltpu.VMEM((blocks, blk, kv_here * HD), bf16),
        pltpu.VMEM((blocks, blk, kv_here * HD), bf16),
        pltpu.VMEM((kv_here, supers, 2 * blk, HD), bf16),
        pltpu.VMEM((kv_here, supers, 2 * blk, HD), bf16),
        pltpu.VMEM((kv_here, supers, HD, 2 * blk), bf16),
        pltpu.VMEM((tasks * 2 * blk, width), f32),
        pltpu.VMEM((chunks, tasks * 2 * blk, width), bf16),
        pltpu.VMEM((2 * (supers + floats), blk, HD), f32),
        pltpu.VMEM((2 * (supers + floats), blk, HD), f32),
        pltpu.VMEM((kv_here, peers, 2 * blk, HD), bf16),
        pltpu.VMEM((kv_here, peers, 2 * blk, HD), bf16),
        pltpu.SemaphoreType.DMA((chunks,)),
        pltpu.SemaphoreType.DMA((chunks,)),
        pltpu.SemaphoreType.DMA((chunks,)),
        pltpu.SemaphoreType.DMA((chunks,)),
        pltpu.SemaphoreType.DMA((chunks,)),
        pltpu.SemaphoreType.DMA((2, cycle)),
        pltpu.SemaphoreType.DMA((2, cycle)),
        pltpu.SemaphoreType.DMA((kv_here, peers)),
        pltpu.SemaphoreType.DMA((kv_here, peers)),
    ]
    pairs = heads * tasks * 2 * blk * blk
    smem = pl.BlockSpec(memory_space=pltpu.SMEM)
    vmem = pl.BlockSpec(memory_space=pltpu.VMEM)
    hbm = pl.BlockSpec(memory_space=pl.ANY)
    return pl.pallas_call(
        kernel,
        out_shape=(
            jax.ShapeDtypeStruct((1, rows, heads * HD), bf16),
            jax.ShapeDtypeStruct((1, rows // tps, KVH * HD), bf16),
            jax.ShapeDtypeStruct((1, rows // tps, KVH * HD), bf16),
        ),
        in_specs=[smem, smem, smem, vmem, vmem, hbm, hbm, hbm],
        out_specs=(hbm, vmem, vmem),
        scratch_shapes=scratch,
        compiler_params=pltpu.CompilerParams(
            collective_id=0, has_side_effects=True, vmem_limit_bytes=56 << 20
        ),
        cost_estimate=pl.CostEstimate(
            flops=5 * 2 * HD * pairs, bytes_accessed=5 * rows * heads * HD * 2,
            transcendentals=pairs,
        ),
    )


def hand_over(*arrays):
    pieces = 8

    count = len(arrays)

    def kernel(*refs):
        sources, targets, held = refs[:count], refs[count:2 * count], refs[2 * count:3 * count]
        in_sems, out_sems = refs[3 * count:]
        inward, outward = [], []
        for source, target, middle in zip(sources, targets, held):
            parts = pieces if source is sources[0] else 1
            step = source.shape[1] // parts
            for i in range(parts):
                part, at = pl.ds(i * step, step), len(inward)
                inward.append(pltpu.make_async_copy(
                    source.at[0, part], middle.at[part], in_sems.at[at]
                ))
                outward.append(pltpu.make_async_copy(
                    middle.at[part], target.at[0, part], out_sems.at[at]
                ))
        for copy in inward:
            copy.start()
        for copy, onward in zip(inward, outward):
            copy.wait()
            onward.start()
        for copy in outward:
            copy.wait()

    hbm = pl.BlockSpec(memory_space=pl.ANY)
    return pl.pallas_call(
        kernel,
        out_shape=tuple(jax.ShapeDtypeStruct(a.shape, a.dtype) for a in arrays),
        in_specs=[hbm] * len(arrays),
        out_specs=(hbm,) * len(arrays),
        scratch_shapes=[pltpu.VMEM(a.shape[1:], a.dtype) for a in arrays]
        + [pltpu.SemaphoreType.DMA((pieces + count - 1,))] * 2,
        compiler_params=pltpu.CompilerParams(vmem_limit_bytes=56 << 20),
    )(*arrays)


def solution(mesh):
    sizes = (mesh.shape["pipe"], mesh.shape["ctx"], mesh.shape["tp"])

    def on_device(
        queries, key_codes, value_codes, kv_scales, saved_out, section_grads, block_order, block_docs
    ):
        call = make_kernel(
            sizes, queries.shape[1], queries.shape[2] // HD, key_codes.shape[2] // HD,
            block_order.shape[0],
        )
        return hand_over(*call(
            block_order, block_docs, kv_scales, key_codes, value_codes, queries, saved_out,
            section_grads,
        ))

    in_specs = (
        P("pipe", "ctx", "tp"),
        P("pipe", "ctx", "tp"),
        P("pipe", "ctx", "tp"),
        P("pipe", "ctx", None),
        P("pipe", "ctx", "tp"),
        P("pipe", "ctx", "tp"),
        P(),
        P(),
    )
    out_specs = (
        P("pipe", "ctx", "tp"),
        P("pipe", ("ctx", "tp"), None),
        P("pipe", ("ctx", "tp"), None),
    )
    return jax.shard_map(
        on_device, mesh=mesh, in_specs=in_specs, out_specs=out_specs, check_vma=False
    )
```
